1024 devices in a mesh: blk: 128 (over z, y), line: 8 (over x, core).
Axes of the slice: x: 4, y: 8, z: 16, core: 2. Of those that a mesh axis runs over, the one named last changes fastest.
Arguments:
- flow_state: float32 [128, 5, 512, 512], P('blk', None, 'line'), may hold values from -6 to 6
- block_owner: int32 [128], replicated, may hold values from 0 to 127, each once
- link_block: int32 [128, 2], replicated, may hold values from 0 to 127, as said below
- link_side: int32 [128, 2], replicated, may hold values from 0 to 1
- rows_live: int32 [128], replicated, may hold values from 256 to 512, as said below
- x_operator: float32 [512, 1024], replicated, may hold values from -0.25 to 0.25
- ghost_operator: float32 [6, 1024], replicated, may hold values from -1.25 to 1.25
- y_operator: float32 [512, 1024], replicated, may hold values from -0.25 to 0.25
- coefficients: float32 [7], replicated, may hold values from 0.2 to 1
Outputs:
- next_state: float32 [128, 5, 512, 512], P('blk', None, 'line')
The draws below stay inside these ranges and needn't reach their ends.
Inputs may be any that keep to these rules, and one draw needn't show every extreme that they name: link_block and link_side join the blocks' faces in pairs: if face m of block b meets face s of block c, then face s of block c meets face m of block b; no block meets itself. `rows_live`: some block has all 512 lines.
All inputs are finite; a program needn't handle non-finite values.
Results may differ from the reference program's by a relative error of at most 0.0003.
Values sent between devices are 32-bit elements; how exact they have to be, the bound alone decides.
A program may use at most 32 MiB of HBM per device.

```python
import jax
import jax.numpy as jnp
from jax import lax

XLEN = 512
YLEN = 512
GHOST = 3
NVAR = 5
BLOCKS = 128


def chain_links(key):
    order = jax.random.permutation(jax.random.fold_in(key, 11), BLOCKS).astype(jnp.int32)
    turned = jax.random.randint(jax.random.fold_in(key, 12), (BLOCKS,), 0, 2).astype(jnp.int32)
    after = jnp.roll(order, -1)
    turn_first = turned[order]
    turn_next = turned[after]
    partner = jnp.zeros((BLOCKS, 2), jnp.int32).at[order, 1 - turn_first].set(after).at[after, turn_next].set(order)
    facing = jnp.zeros((BLOCKS, 2), jnp.int32).at[order, 1 - turn_first].set(turn_next).at[after, turn_next].set(1 - turn_first)
    return (partner, facing)


def draw_link_block(key, part):
    return chain_links(key)[0]


def draw_link_side(key, part):
    return chain_links(key)[1]


def draw_rows_live(key, part):
    counts = jax.random.randint(jax.random.fold_in(key, 21), (BLOCKS,), YLEN // 2, YLEN + 1).astype(jnp.int32)
    fullest = jax.random.randint(jax.random.fold_in(key, 22), (), 0, BLOCKS)
    return counts.at[fullest].set(YLEN)


def steps_of(key, dims, shards, low, high):
    level = 1.0
    for axis_at, blocks in shards:
        heights = jax.random.uniform(jax.random.fold_in(jax.random.fold_in(key, 6), axis_at), (blocks,), jnp.float32, low / len(shards), high / len(shards))
        level = level * jnp.repeat(jnp.exp(heights), dims[axis_at] // blocks).reshape((-1,) + (1,) * (len(dims) - 1 - axis_at))
    return level


def noise(own_key, shape, scale, reach, split=(), kind=jnp.bfloat16):
    values = scale * jax.random.normal(own_key, shape, jnp.float32)
    if split:
        values = values * steps_of(own_key, shape, split, -0.22, 0.18)
    return jnp.clip(values, -reach, reach).astype(kind)


def setup_inputs(seed: int = 0) -> dict:
    arg_keys = jax.random.split(jax.random.key(seed), 10)
    flow_state = noise(arg_keys[0], (BLOCKS, NVAR, YLEN, XLEN), 1.0, 6.0, ((0, 128), (2, 8)), jnp.float32)
    block_owner = jax.random.permutation(arg_keys[1], BLOCKS).astype(jnp.int32)
    link_block = draw_link_block(jax.random.fold_in(arg_keys[9], 71), 0)
    link_side = draw_link_side(jax.random.fold_in(arg_keys[9], 71), 0)
    rows_live = draw_rows_live(jax.random.fold_in(arg_keys[9], 71), 0)
    x_operator = noise(arg_keys[5], (XLEN, 2 * XLEN), XLEN ** -0.5, 0.25, (), jnp.float32)
    ghost_operator = noise(arg_keys[6], (2 * GHOST, 2 * XLEN), (8 * GHOST) ** -0.5, 1.25, (), jnp.float32)
    y_operator = noise(arg_keys[7], (YLEN, 2 * YLEN), YLEN ** -0.5, 0.25, (), jnp.float32)
    coefficients = jnp.clip(jax.random.uniform(arg_keys[8], (NVAR + 2,), jnp.float32, 0.2, 1.0), 0.2, 1.0)
    return dict(flow_state=flow_state, block_owner=block_owner, link_block=link_block, link_side=link_side, rows_live=rows_live, x_operator=x_operator, ghost_operator=ghost_operator, y_operator=y_operator, coefficients=coefficients)


highest = lax.Precision.HIGHEST
section_step = 0.3


def reference(flow_state, block_owner, link_block, link_side, rows_live, x_operator, ghost_operator, y_operator, coefficients):
    block_count = block_owner.shape[0]
    slots = jnp.arange(block_count, dtype=jnp.int32)
    block_of = jnp.sum(slots[:, None] * (block_owner[:, None] == slots[None, :]).astype(jnp.int32), axis=0).astype(jnp.int32)
    live_rows = rows_live[block_of]
    y_index = jnp.arange(YLEN, dtype=jnp.int32)
    live_mask = (y_index[None, :] < live_rows[:, None]).astype(jnp.float32)
    masked = flow_state * live_mask[:, None, :, None]
    low_planes = masked[..., :GHOST]
    high_planes = masked[..., XLEN - GHOST:]
    flip_sign = jnp.array([-1.0, 1.0, 1.0, 1.0, 1.0], dtype=jnp.float32)[:, None, None]
    nu_values = coefficients[:NVAR][:, None, None]

    def ghost_side(my_block, my_side):
        partner = link_block[my_block, my_side]
        far_side = link_side[my_block, my_side]
        partner_slot = block_owner[partner]
        chosen = jnp.where(far_side == 0, low_planes[partner_slot], high_planes[partner_slot])
        return jnp.where(far_side == my_side, chosen[..., ::-1] * flip_sign, chosen)

    def advance(slot_index):
        my_block = block_of[slot_index]
        ghost_planes = jnp.concatenate([ghost_side(my_block, 0), ghost_side(my_block, 1)], axis=-1)
        values = masked[slot_index]
        x_parts = jnp.einsum("vyx,xk->vyk", values, x_operator, precision=highest)
        x_parts = x_parts + jnp.einsum("vyg,gk->vyk", ghost_planes, ghost_operator, precision=highest)
        y_parts = jnp.einsum("vyx,yk->vkx", values, y_operator, precision=highest)
        dx_part = x_parts[..., :XLEN]
        dxx_part = x_parts[..., XLEN:]
        dy_part = y_parts[:, :YLEN]
        dyy_part = y_parts[:, YLEN:]
        rhs_terms = -(values[0][None] * dx_part + values[1][None] * dy_part) + nu_values * (dxx_part + dyy_part)
        buoyancy = coefficients[NVAR] * values[3] + coefficients[NVAR + 1] * values[4]
        picker = (jnp.arange(NVAR) == 1).astype(jnp.float32)[:, None, None]
        rhs_terms = rhs_terms + picker * buoyancy[None]
        return (values + section_step * rhs_terms) * live_mask[slot_index][None, :, None]

    return lax.map(advance, slots)
```

```python
import functools

import jax
import jax.numpy as jnp
from jax import lax
from jax.experimental import pallas as pl
from jax.experimental.pallas import tpu as pltpu
from jax.sharding import PartitionSpec as P

NY = 8
STEP = 0.3
MESH = pl.DeviceIdType.MESH
F32 = jnp.float32
BF16 = jnp.bfloat16
PEERS = ((1, 0), (3, 0), (1, 1), (3, 1), (2, 0), (2, 1), (0, 1))


def split(value):
    high = value.astype(BF16)
    return high, (value - high.astype(F32)).astype(BF16)


def mm(a, b):
    return jnp.dot(a, b, preferred_element_type=F32)


def kernel(
    nz,
    ny,
    flow,
    owner_h,
    link_block_h,
    link_side_h,
    rows_live_h,
    xop_h,
    gop_h,
    yop_h,
    coef_h,
    out,
    m,
    owner_v,
    link_block_v,
    link_side_v,
    rows_live_v,
    coef,
    gop,
    xop,
    yop,
    xh,
    xl,
    yth,
    ytl,
    mh,
    ml,
    s_ab,
    s_c,
    r_ab,
    r_c,
    t_ab,
    t_c,
    b_ab,
    b_c,
    vv,
    qcat,
    res,
    res2,
    acc,
    face,
    gz,
    sy,
    ry,
    load_sem,
    fs,
    fr,
    bs,
    br,
    zs,
    zr,
    ys,
    yr,
):
    line = lax.axis_index("line")
    slot = lax.axis_index("blk")
    chip, core = line // 2, lax.rem(line, 2)
    z, y = slot // ny, lax.rem(slot, ny)

    def peer(ahead, other):
        return lax.rem(chip + ahead, 4) * 2 + lax.rem(core + other, 2)

    def z_peer(d):
        return lax.rem(z + d, nz) * ny + y

    def y_peer(d):
        return z * ny + lax.rem(y + d, ny)

    barrier = pltpu.get_barrier_semaphore()
    for ahead, other in PEERS:
        pl.semaphore_signal(barrier, inc=1, device_id={"line": peer(ahead, other)}, device_id_type=MESH)

    @pl.loop(1, nz)
    def _(d):
        pl.semaphore_signal(barrier, inc=1, device_id={"blk": z_peer(d)}, device_id_type=MESH)

    @pl.loop(1, ny)
    def _(d):
        pl.semaphore_signal(barrier, inc=1, device_id={"blk": y_peer(d)}, device_id_type=MESH)

    loads = [
        pltpu.make_async_copy(a, b, load_sem.at[i])
        for i, (a, b) in enumerate(
            (
                (rows_live_h, rows_live_v),
                (owner_h, owner_v),
                (flow, m),
                (link_block_h, link_block_v),
                (link_side_h, link_side_v),
                (coef_h, coef),
                (gop_h, gop),
                (yop_h, yop),
                (xop_h, xop),
            )
        )
    ]
    for load in loads:
        load.start()
    loads[0].wait()
    loads[1].wait()

    lanes = lax.broadcasted_iota(jnp.int32, (64, 128), 1)
    lo = lanes < 64
    mine = owner_v[...] == slot
    live_rows = jnp.sum(jnp.where(mine, rows_live_v[...].astype(F32), 0.0), axis=1, keepdims=True)
    row_id = (lax.broadcasted_iota(jnp.int32, (64, 128), 0) + line * 64).astype(F32)
    live = (row_id < live_rows).astype(F32)
    loads[2].wait()

    for pair, (first, second) in enumerate(((1, 0), (2, 3))):
        for c in range(4):
            cols = slice(128 * c, 128 * c + 128)
            a = m[first, :, cols] * live
            b = m[second, :, cols] * live
            m[first, :, cols] = a
            m[second, :, cols] = b
            s_ab[pair, 2 * c] = jnp.where(lo, a, pltpu.roll(b, 64, 1))
            s_ab[pair, 2 * c + 1] = jnp.where(lo, pltpu.roll(a, 64, 1), b)
    lo32 = lo[:32]
    for c in range(4):
        cols = slice(128 * c, 128 * c + 128)
        a = m[4, :, cols] * live
        m[4, :, cols] = a
        s_c[2 * c] = jnp.where(lo32, a[:32], pltpu.roll(a[32:], 64, 1))
        s_c[2 * c + 1] = jnp.where(lo32, pltpu.roll(a[:32], 64, 1), a[32:])

    planes = []
    for v in range(5):
        planes.append(jnp.where(lanes < 3, m[v, :, 0:128], pltpu.roll(m[v, :, 384:512], 6, 1)))
    planes.append(jnp.zeros((64, 128), F32))
    for j in range(3):
        both = jnp.concatenate([planes[2 * j], planes[2 * j + 1]], axis=0)
        face[:, 128 * j : 128 * j + 128] = jnp.transpose(both)[:8]

    pl.semaphore_wait(barrier, len(PEERS) + nz - 1 + ny - 1)

    here = pl.ds(pl.multiple_of(line * 64, 64), 64)

    def forward(chunk, i):
        ahead, other = PEERS[i]
        to = peer(ahead, other)
        if chunk < 2:
            source, target = s_ab.at[chunk, to], r_ab.at[chunk, here]
        else:
            source, target = s_c.at[to], r_c.at[line]
        return pltpu.make_async_remote_copy(
            src_ref=source,
            dst_ref=target,
            send_sem=fs.at[chunk, i],
            recv_sem=fr.at[chunk, i],
            device_id={"line": to},
            device_id_type=MESH,
        )

    def backward(chunk, i):
        ahead, other = PEERS[i]
        to = peer(ahead, other)
        if chunk < 2:
            source = t_ab.at[chunk, pl.ds(pl.multiple_of(to * 64, 64), 64)]
            target = b_ab.at[chunk, line]
        else:
            source, target = t_c.at[to], b_c.at[line]
        return pltpu.make_async_remote_copy(
            src_ref=source,
            dst_ref=target,
            send_sem=bs.at[chunk, i],
            recv_sem=br.at[chunk, i],
            device_id={"line": to},
            device_id_type=MESH,
        )

    def z_copy(d):
        return pltpu.make_async_remote_copy(
            src_ref=face,
            dst_ref=gz.at[z],
            send_sem=zs.at[d],
            recv_sem=zr.at[d],
            device_id={"blk": z_peer(d)},
            device_id_type=MESH,
        )

    def y_copy(d):
        return pltpu.make_async_remote_copy(
            src_ref=sy.at[lax.rem(y + d, ny)],
            dst_ref=ry.at[y],
            send_sem=ys.at[d],
            recv_sem=yr.at[d],
            device_id={"blk": y_peer(d)},
            device_id_type=MESH,
        )

    for i in range(7):
        forward(0, i).start()

    @pl.loop(1, nz)
    def _(d):
        z_copy(d).start()

    for chunk in (1, 2):
        for i in range(7):
            forward(chunk, i).start()
    gz[z] = face[...]
    r_ab[0, here] = s_ab[0, line]
    r_ab[1, here] = s_ab[1, line]
    r_c[line] = s_c[line]

    loads[7].wait()

    @pl.loop(0, 8)
    def _(i):
        rows = pl.ds(pl.multiple_of(i * 128, 128), 128)
        for j in range(4):
            block = jnp.transpose(yop[128 * j : 128 * j + 128, rows])
            high, low = split(block)
            yth[rows, 128 * j : 128 * j + 128] = high
            ytl[rows, 128 * j : 128 * j + 128] = low

    loads[3].wait()
    loads[4].wait()
    peers_row = lax.broadcasted_iota(jnp.int32, (ny, nz * ny), 0) + z * ny
    lane_row = lax.broadcasted_iota(jnp.int32, (ny, nz * ny), 1).astype(F32)
    owner = owner_v[...]
    owner_f = owner.astype(F32)
    hot = owner == peers_row
    wanted = []
    for side in range(2):
        partner = jnp.sum(
            jnp.where(hot, link_block_v[side : side + 1, :].astype(F32), 0.0), axis=1, keepdims=True
        )
        far = jnp.sum(
            jnp.where(hot, link_side_v[side : side + 1, :].astype(F32), 0.0), axis=1, keepdims=True
        )
        source = jnp.sum(jnp.where(lane_row == partner, owner_f, 0.0), axis=1, keepdims=True)
        wanted.append((source, far))

    @pl.loop(1, nz)
    def _(d):
        z_copy(d).wait_recv()

    plane_row = lax.broadcasted_iota(jnp.int32, (8, 384), 0)
    for p in range(ny):
        parts = []
        for side in range(2):
            source = jnp.broadcast_to(wanted[side][0][p : p + 1], (8, 384))
            far = jnp.broadcast_to(wanted[side][1][p : p + 1], (8, 384))
            total = jnp.zeros((8, 384), F32)
            for zz in range(nz):
                code = (y + zz * ny).astype(F32)
                total = total + jnp.where(source == code, gz[zz], 0.0)
            parts.append(jnp.where(far < 0.5, total, pltpu.roll(total, 5, 0)))
        sy[p] = jnp.where(plane_row < 3, parts[0], pltpu.roll(parts[1], 3, 0))

    @pl.loop(1, ny)
    def _(d):
        y_copy(d).start()

    ry[y] = sy[y]

    loads[5].wait()
    nu = [coef[v] for v in range(5)]

    def y_pair(pair, nu_first, nu_second):
        nu_lane = STEP * jnp.where(lo, nu_first, nu_second)
        high, low = split(r_ab[pair])
        qcat[:, :128] = high
        qcat[:, 128:] = low
        res[...] = mm(yth[...], qcat[...])
        res2[...] = mm(ytl[...], qcat[:, :128])

        @pl.loop(0, 8)
        def _(i):
            a = pl.ds(pl.multiple_of(i * 64, 64), 64)
            b = pl.ds(pl.multiple_of(i * 64 + 512, 64), 64)
            dy = res[a, :128] + res[a, 128:] + res2[a]
            dyy = res[b, :128] + res[b, 128:] + res2[b]
            t_ab[pair, a] = nu_lane * dyy - vv[a] * dy

    for i in range(7):
        forward(0, i).wait_recv()
    first = r_ab[0]
    lo_all = lax.broadcasted_iota(jnp.int32, (512, 128), 1) < 64
    vv[...] = STEP * jnp.where(lo_all, first, pltpu.roll(first, 64, 1))
    y_pair(0, nu[1], nu[0])
    for i in range(7):
        backward(0, i).start()
    b_ab[0, line] = t_ab[0, here]

    for i in range(7):
        forward(1, i).wait_recv()
    y_pair(1, nu[2], nu[3])
    for i in range(7):
        backward(1, i).start()
    b_ab[1, line] = t_ab[1, here]

    for i in range(7):
        forward(2, i).wait_recv()
    for s in range(8):
        part = r_c[s]
        turned = pltpu.roll(part, 64, 1)
        for half, (keep, other) in enumerate(((part, turned), (turned, part))):
            high = keep.astype(BF16).astype(F32)
            low = other - other.astype(BF16).astype(F32)
            rows = slice(64 * s + 32 * half, 64 * s + 32 * half + 32)
            qcat[rows, :128] = jnp.where(lo32, high, low).astype(BF16)
    res2[...] = mm(yth[...], qcat[:, :128]) + mm(ytl[...], qcat[:, :128])

    @pl.loop(0, 8)
    def _(i):
        a = pl.ds(pl.multiple_of(i * 64, 64), 64)
        b = pl.ds(pl.multiple_of(i * 64 + 512, 64), 64)
        dy = res2[a] + pltpu.roll(res2[a], 64, 1)
        dyy = res2[b] + pltpu.roll(res2[b], 64, 1)
        term = (STEP * nu[4]) * dyy - vv[a] * dy
        t_c[i] = jnp.where(lo32, term[:32], term[32:])

    for i in range(7):
        backward(2, i).start()
    b_c[line] = t_c[line]

    own = []
    for side in range(2):
        own.append(
            jnp.sum(jnp.where(mine, link_side_v[side : side + 1, :].astype(F32), 0.0), axis=1, keepdims=True)
        )

    @pl.loop(1, ny)
    def _(d):
        y_copy(d).wait_recv()

    ghost = ry[0]
    for p in range(1, ny):
        ghost = ghost + ry[p]
    flip = jnp.where(plane_row < 3, 1.0 - own[0], own[1])
    turned = jnp.where(
        (plane_row == 0) | (plane_row == 3),
        pltpu.roll(ghost, 6, 0),
        jnp.where((plane_row == 2) | (plane_row == 5), pltpu.roll(ghost, 2, 0), ghost),
    )
    column = lax.broadcasted_iota(jnp.int32, (8, 384), 1)
    turned = jnp.where(column < 64, -turned, turned)
    ghost = jnp.where(flip > 0.5, turned, ghost)
    ghost = jnp.where(plane_row < 6, ghost, 0.0)
    ghost_high = ghost.astype(BF16).astype(F32)
    stack = jnp.concatenate([ghost_high, ghost - ghost_high, ghost_high, jnp.zeros((104, 384), F32)], axis=0)
    ghost_t = jnp.concatenate(
        [jnp.transpose(stack[:, 128 * j : 128 * j + 128]) for j in range(3)], axis=0
    )[:320].astype(BF16)
    loads[6].wait()
    g_op = jnp.concatenate([gop[...], jnp.zeros((2, 1024), F32)], axis=0)
    g_high = g_op.astype(BF16).astype(F32)
    g_stack = jnp.concatenate(
        [g_high, g_high, g_op - g_high, jnp.zeros((104, 1024), F32)], axis=0
    ).astype(BF16)
    gop_stack = g_stack

    loads[8].wait()

    @pl.loop(0, 8)
    def _(i):
        rows = pl.ds(pl.multiple_of(i * 64, 64), 64)
        high, low = split(xop[rows])
        xh[rows] = high
        xl[rows] = low

    for v in range(5):
        high, low = split(m[v])
        mh[64 * v : 64 * v + 64] = high
        ml[64 * v : 64 * v + 64] = low
    for n in range(2):
        deriv = []
        for o in range(2):
            cols = slice(512 * o + 256 * n, 512 * o + 256 * n + 256)
            deriv.append(
                mm(mh[...], xh[:, cols])
                + mm(ml[...], xh[:, cols])
                + mm(mh[...], xl[:, cols])
                + mm(ghost_t, gop_stack[:, cols])
            )
        cols = slice(256 * n, 256 * n + 256)
        u = STEP * m[0, :, cols]
        for v in range(5):
            rows = slice(64 * v, 64 * v + 64)
            term = m[v, :, cols] + (STEP * nu[v]) * deriv[1][rows] - u * deriv[0][rows]
            if v == 1:
                term = term + (STEP * coef[5]) * m[3, :, cols] + (STEP * coef[6]) * m[4, :, cols]
            acc[v, :, cols] = term

    for pair, (one, two) in enumerate(((1, 0), (2, 3))):
        for i in range(7):
            backward(pair, i).wait_recv()
        for c in range(4):
            cols = slice(128 * c, 128 * c + 128)
            a, b = b_ab[pair, 2 * c], b_ab[pair, 2 * c + 1]
            out[one, :, cols] = live * (acc[one, :, cols] + jnp.where(lo, a, pltpu.roll(b, 64, 1)))
            out[two, :, cols] = live * (acc[two, :, cols] + jnp.where(lo, pltpu.roll(a, 64, 1), b))
    for i in range(7):
        backward(2, i).wait_recv()
    for c in range(4):
        cols = slice(128 * c, 128 * c + 128)
        a, b = b_c[2 * c], b_c[2 * c + 1]
        top = jnp.where(lo32, a, pltpu.roll(b, 64, 1))
        bottom = jnp.where(lo32, pltpu.roll(a, 64, 1), b)
        out[4, :32, cols] = live[:32] * (acc[4, :32, cols] + top)
        out[4, 32:, cols] = live[32:] * (acc[4, 32:, cols] + bottom)

    for chunk in range(3):
        for i in range(7):
            forward(chunk, i).wait_send()
            backward(chunk, i).wait_send()

    @pl.loop(1, nz)
    def _(d):
        z_copy(d).wait_send()

    @pl.loop(1, ny)
    def _(d):
        y_copy(d).wait_send()


def on_device(
    nz,
    ny,
    flow_state,
    block_owner,
    link_block,
    link_side,
    rows_live,
    x_operator,
    ghost_operator,
    y_operator,
    coefficients,
):
    any_spec = pl.BlockSpec(memory_space=pltpu.HBM)
    dma = pltpu.SemaphoreType.DMA
    blocks = nz * ny
    result = pl.pallas_call(
        functools.partial(kernel, nz, ny),
        out_shape=jax.ShapeDtypeStruct((5, 64, 512), F32),
        in_specs=[any_spec] * 9,
        out_specs=pl.BlockSpec(memory_space=pltpu.VMEM),
        scratch_shapes=[
            pltpu.VMEM((5, 64, 512), F32),
            pltpu.VMEM((1, blocks), jnp.int32),
            pltpu.VMEM((2, blocks), jnp.int32),
            pltpu.VMEM((2, blocks), jnp.int32),
            pltpu.VMEM((1, blocks), jnp.int32),
            pltpu.SMEM((7,), F32),
            pltpu.VMEM((6, 1024), F32),
            pltpu.VMEM((512, 1024), F32),
            pltpu.VMEM((512, 1024), F32),
            pltpu.VMEM((512, 1024), BF16),
            pltpu.VMEM((512, 1024), BF16),
            pltpu.VMEM((1024, 512), BF16),
            pltpu.VMEM((1024, 512), BF16),
            pltpu.VMEM((320, 512), BF16),
            pltpu.VMEM((320, 512), BF16),
            pltpu.VMEM((2, 8, 64, 128), F32),
            pltpu.VMEM((8, 32, 128), F32),
            pltpu.VMEM((2, 512, 128), F32),
            pltpu.VMEM((8, 32, 128), F32),
            pltpu.VMEM((2, 512, 128), F32),
            pltpu.VMEM((8, 32, 128), F32),
            pltpu.VMEM((2, 8, 64, 128), F32),
            pltpu.VMEM((8, 32, 128), F32),
            pltpu.VMEM((512, 128), F32),
            pltpu.VMEM((512, 256), BF16),
            pltpu.VMEM((1024, 256), F32),
            pltpu.VMEM((1024, 128), F32),
            pltpu.VMEM((5, 64, 512), F32),
            pltpu.VMEM((8, 384), F32),
            pltpu.VMEM((nz, 8, 384), F32),
            pltpu.VMEM((ny, 8, 384), F32),
            pltpu.VMEM((ny, 8, 384), F32),
            dma((9,)),
            dma((3, 7)),
            dma((3, 7)),
            dma((3, 7)),
            dma((3, 7)),
            dma((nz,)),
            dma((nz,)),
            dma((ny,)),
            dma((ny,)),
        ],
        compiler_params=pltpu.CompilerParams(
            collective_id=0, has_side_effects=True, vmem_limit_bytes=56 * 1024 * 1024
        ),
        cost_estimate=pl.CostEstimate(flops=2 * 10**9, bytes_accessed=6 * 10**6, transcendentals=0),
    )(
        flow_state[0],
        block_owner[None],
        link_block.T,
        link_side.T,
        rows_live[None],
        x_operator,
        ghost_operator,
        y_operator,
        coefficients,
    )
    return result[None]


def solution(mesh):
    blocks = mesh.shape["blk"]
    ny = min(NY, blocks // 2)
    return jax.shard_map(
        functools.partial(on_device, blocks // ny, ny),
        mesh=mesh,
        in_specs=(P("blk", None, "line", None), P(), P(), P(), P(), P(), P(), P(), P()),
        out_specs=P("blk", None, "line", None),
        check_vma=False,
    )
```

```python
import functools

import jax
import jax.numpy as jnp
from jax import lax
from jax.experimental import pallas as pl
from jax.experimental.pallas import tpu as pltpu
from jax.sharding import PartitionSpec as P

NY = 8
STEP = 0.3
MESH = pl.DeviceIdType.MESH
F32 = jnp.float32
BF16 = jnp.bfloat16
PEERS = ((1, 0), (3, 0), (1, 1), (3, 1), (2, 0), (2, 1), (0, 1))


def split(value):
    high = value.astype(BF16)
    return high, (value - high.astype(F32)).astype(BF16)


def mm(a, b):
    return jnp.dot(a, b, preferred_element_type=F32)


def kernel(
    nz,
    ny,
    z_late,
    flow,
    owner_h,
    link_block_h,
    link_side_h,
    rows_live_h,
    xop_h,
    gop_h,
    yop_h,
    coef_h,
    out,
    m,
    owner_v,
    link_block_v,
    link_side_v,
    rows_live_v,
    coef,
    gop,
    xop,
    yop,
    xh,
    xl,
    yth,
    ytl,
    mh,
    ml,
    s_ab,
    s_c,
    r_ab,
    r_c,
    t_ab,
    t_c,
    b_ab,
    b_c,
    vv,
    qcat,
    res,
    res2,
    acc,
    face,
    gz,
    sy,
    ry,
    load_sem,
    fs,
    fr,
    bs,
    br,
    zs,
    zr,
    ys,
    yr,
    ready,
    gstack,
):
    line = lax.axis_index("line")
    slot = lax.axis_index("blk")
    chip, core = line // 2, lax.rem(line, 2)
    z, y = slot // ny, lax.rem(slot, ny)

    def peer(ahead, other):
        return lax.rem(chip + ahead, 4) * 2 + lax.rem(core + other, 2)

    is_first = (slot == 0) & (line == 0)
    late_line = (slot == 0) & (line != 0)
    z_special = (y == 0) & (line == 0)
    y_special = (z == 0) & (line == 0) & (y != 0)

    def z_start(zz):
        usual = jnp.where(zz < 8, 15 * zz, 88 + 4 * zz)
        return jnp.where(z_special & (zz == 0), z_late, usual)

    my_z = z_start(z)

    def z_close(zz):
        near = jnp.abs(z_start(zz) - my_z) <= 10
        return near & jnp.logical_not(z_special & ((zz == 0) | (z == 0)))

    def z_now(zz):
        return (zz != z) & ((z_start(zz) < my_z) | z_close(zz))

    def z_after(zz, least, most):
        gap = z_start(zz) - my_z
        return (gap > least) & (gap <= most) & jnp.logical_not(z_close(zz))

    barrier = pltpu.get_barrier_semaphore()

    @pl.when(jnp.logical_not(is_first))
    def _():
        for ahead, other in PEERS:
            pl.semaphore_signal(
                barrier, inc=1, device_id={"line": peer(ahead, other)}, device_id_type=MESH
            )

    waits = len(PEERS) - jnp.where(late_line, 1, 0) + ny - 1 - jnp.where(y_special, 1, 0)
    for zz in range(nz):
        waits += jnp.where(z_now(zz), 1, 0)

    @pl.loop(0, nz)
    def _(zz):
        @pl.when((zz != z) & ((z_start(zz) > my_z) | z_close(zz)))
        def _():
            pl.semaphore_signal(barrier, inc=1, device_id={"blk": zz * ny + y}, device_id_type=MESH)

    @pl.loop(0, ny)
    def _(yy):
        @pl.when((yy != y) & jnp.logical_not(is_first))
        def _():
            pl.semaphore_signal(barrier, inc=1, device_id={"blk": z * ny + yy}, device_id_type=MESH)

    loads = [
        pltpu.make_async_copy(a, b, load_sem.at[i])
        for i, (a, b) in enumerate(
            (
                (rows_live_h, rows_live_v),
                (owner_h, owner_v),
                (flow, m),
                (link_block_h, link_block_v),
                (link_side_h, link_side_v),
                (coef_h, coef),
                (gop_h, gop),
                (yop_h, yop),
                (xop_h, xop),
            )
        )
    ]
    for load in loads:
        load.start()

    @pl.when(is_first)
    def _():
        pl.semaphore_wait(barrier, waits)
        for ahead, other in PEERS:
            pl.semaphore_signal(
                ready, inc=1, device_id={"line": peer(ahead, other)}, device_id_type=MESH
            )

        @pl.loop(1, ny)
        def _(yy):
            pl.semaphore_signal(ready, inc=1, device_id={"blk": z * ny + yy}, device_id_type=MESH)

    loads[0].wait()
    loads[1].wait()

    lanes = lax.broadcasted_iota(jnp.int32, (64, 128), 1)
    lo = lanes < 64
    mine = owner_v[...] == slot
    live_rows = jnp.sum(jnp.where(mine, rows_live_v[...].astype(F32), 0.0), axis=1, keepdims=True)
    row_id = (lax.broadcasted_iota(jnp.int32, (64, 128), 0) + line * 64).astype(F32)
    live = (row_id < live_rows).astype(F32)
    loads[2].wait()

    for pair, (first, second) in enumerate(((1, 0), (2, 3))):
        for c in range(4):
            cols = slice(128 * c, 128 * c + 128)
            a = m[first, :, cols] * live
            b = m[second, :, cols] * live
            m[first, :, cols] = a
            m[second, :, cols] = b
            s_ab[pair, 2 * c] = jnp.where(lo, a, pltpu.roll(b, 64, 1))
            s_ab[pair, 2 * c + 1] = jnp.where(lo, pltpu.roll(a, 64, 1), b)
    lo32 = lo[:32]
    for c in range(4):
        cols = slice(128 * c, 128 * c + 128)
        a = m[4, :, cols] * live
        m[4, :, cols] = a
        s_c[2 * c] = jnp.where(lo32, a[:32], pltpu.roll(a[32:], 64, 1))
        s_c[2 * c + 1] = jnp.where(lo32, pltpu.roll(a[:32], 64, 1), a[32:])

    planes = []
    for v in range(5):
        planes.append(jnp.where(lanes < 3, m[v, :, 0:128], pltpu.roll(m[v, :, 384:512], 6, 1)))
    last = planes[4]
    for v, moves in enumerate(((6, 6), (3, 3), (4, None), (1, None))):
        for lane, move in zip((6, 7), moves):
            if move is not None:
                planes[v] = jnp.where(lanes == lane, pltpu.roll(last, move, 1), planes[v])
    for j in range(2):
        both = jnp.concatenate([planes[2 * j], planes[2 * j + 1]], axis=0)
        face[:, 128 * j : 128 * j + 128] = jnp.transpose(both)[:8]

    @pl.when(jnp.logical_not(is_first))
    def _():
        pl.semaphore_wait(barrier, waits)

    here = pl.ds(pl.multiple_of(line * 64, 64), 64)

    def forward(chunk, i):
        ahead, other = PEERS[i]
        to = peer(ahead, other)
        if chunk < 2:
            source, target = s_ab.at[chunk, to], r_ab.at[chunk, here]
        else:
            source, target = s_c.at[to], r_c.at[line]
        return pltpu.make_async_remote_copy(
            src_ref=source,
            dst_ref=target,
            send_sem=fs.at[chunk, i],
            recv_sem=fr.at[chunk, i],
            device_id={"line": to},
            device_id_type=MESH,
        )

    def backward(chunk, i):
        ahead, other = PEERS[i]
        to = peer(ahead, other)
        if chunk < 2:
            source = t_ab.at[chunk, pl.ds(pl.multiple_of(to * 64, 64), 64)]
            target = b_ab.at[chunk, line]
        else:
            source, target = t_c.at[to], b_c.at[line]
        return pltpu.make_async_remote_copy(
            src_ref=source,
            dst_ref=target,
            send_sem=bs.at[chunk, i],
            recv_sem=br.at[chunk, i],
            device_id={"line": to},
            device_id_type=MESH,
        )

    def z_copy(zz, sender):
        return pltpu.make_async_remote_copy(
            src_ref=face,
            dst_ref=gz.at[sender],
            send_sem=zs.at[zz],
            recv_sem=zr.at[sender],
            device_id={"blk": zz * ny + y},
            device_id_type=MESH,
        )

    def y_copy(yy, sender):
        return pltpu.make_async_remote_copy(
            src_ref=sy.at[yy],
            dst_ref=ry.at[sender],
            send_sem=ys.at[yy],
            recv_sem=yr.at[sender],
            device_id={"blk": z * ny + yy},
            device_id_type=MESH,
        )

    def is_late(i):
        return late_line & (peer(*PEERS[i]) == 0)

    def send_forward(chunk, i):
        @pl.when(jnp.logical_not(is_late(i)))
        def _():
            forward(chunk, i).start()

    @pl.loop(0, nz)
    def _(zz):
        @pl.when(z_now(zz))
        def _():
            z_copy(zz, z).start()

    for chunk in range(3):
        for i in range(7):
            send_forward(chunk, i)

    gz[z] = face[...]
    r_ab[0, here] = s_ab[0, line]
    r_ab[1, here] = s_ab[1, line]
    r_c[line] = s_c[line]

    loads[7].wait()

    @pl.loop(0, 8)
    def _(i):
        rows = pl.ds(pl.multiple_of(i * 128, 128), 128)
        for j in range(4):
            block = jnp.transpose(yop[128 * j : 128 * j + 128, rows])
            high, low = split(block)
            yth[rows, 128 * j : 128 * j + 128] = high
            ytl[rows, 128 * j : 128 * j + 128] = low

    loads[3].wait()
    loads[4].wait()
    peers_row = lax.broadcasted_iota(jnp.int32, (ny, nz * ny), 0) + z * ny
    lane_row = lax.broadcasted_iota(jnp.int32, (ny, nz * ny), 1).astype(F32)
    owner = owner_v[...]
    owner_f = owner.astype(F32)
    hot = owner == peers_row
    wanted = []
    for side in range(2):
        partner = jnp.sum(
            jnp.where(hot, link_block_v[side : side + 1, :].astype(F32), 0.0), axis=1, keepdims=True
        )
        far = jnp.sum(
            jnp.where(hot, link_side_v[side : side + 1, :].astype(F32), 0.0), axis=1, keepdims=True
        )
        source = jnp.sum(jnp.where(lane_row == partner, owner_f, 0.0), axis=1, keepdims=True)
        wanted.append((source, far))

    own = []
    for side in range(2):
        own.append(
            jnp.sum(jnp.where(mine, link_side_v[side : side + 1, :].astype(F32), 0.0), axis=1, keepdims=True)
        )

    loads[6].wait()
    g_op = jnp.concatenate([gop[...], jnp.zeros((2, 1024), F32)], axis=0)
    g_high = g_op.astype(BF16).astype(F32)
    gstack[...] = jnp.concatenate(
        [g_high, g_high, g_op - g_high, jnp.zeros((104, 1024), F32)], axis=0
    ).astype(BF16)

    plane_row = lax.broadcasted_iota(jnp.int32, (8, 384), 0)
    wide_row = plane_row[:, :256]
    half = lax.rem(lax.broadcasted_iota(jnp.int32, (8, 256), 1), 128) // 64
    of_face = [
        ((wide_row >= 3 * f) & (wide_row < 3 * f + 3)) | ((wide_row >= 6) & (half == f))
        for f in range(2)
    ]

    def answer(least, most):
        @pl.loop(1, nz + 1)
        def _(step):
            zz = lax.rem(step, nz)

            @pl.when(z_after(zz, least, most))
            def _():
                z_copy(zz, zz).wait_recv()
                z_copy(zz, z).start()

    def ghost_stage():
        answer(60, 1000)

        @pl.loop(0, nz)
        def _(zz):
            @pl.when(z_now(zz))
            def _():
                z_copy(zz, zz).wait_recv()

        for p in range(ny):
            message = jnp.zeros((8, 256), F32)
            for side in range(2):
                source = jnp.broadcast_to(wanted[side][0][p : p + 1], (8, 256))
                far = jnp.broadcast_to(wanted[side][1][p : p + 1], (8, 256))
                total = jnp.zeros((8, 256), F32)
                for zz in range(nz):
                    code = (y + zz * ny).astype(F32)
                    total = total + jnp.where(source == code, gz[zz], 0.0)
                halves = jnp.concatenate(
                    [pltpu.roll(total[:, 128 * j : 128 * j + 128], 64, 1) for j in range(2)], axis=1
                )
                swapped = jnp.where(wide_row < 6, pltpu.roll(total, 3 if side else 5, 0), halves)
                chosen = jnp.where(jnp.abs(far - side) < 0.5, total, swapped)
                message = jnp.where(of_face[side], chosen, message)
            sy[p] = message

        @pl.when(y_special)
        def _():
            pl.semaphore_wait(ready, 1)

        @pl.loop(0, ny)
        def _(yy):
            @pl.when(yy != y)
            def _():
                y_copy(yy, y).start()

        ry[y] = sy[y]

    @pl.when(late_line)
    def _():
        pl.semaphore_wait(ready, 1)

    for chunk in range(3):
        for i in range(7):

            @pl.when(is_late(i))
            def _():
                forward(chunk, i).start()

    loads[5].wait()
    nu = [coef[v] for v in range(5)]

    def y_pair(pair, nu_first, nu_second):
        nu_lane = STEP * jnp.where(lo, nu_first, nu_second)
        high, low = split(r_ab[pair])
        qcat[:, :128] = high
        qcat[:, 128:] = low
        res[...] = mm(yth[...], qcat[...])
        res2[...] = mm(ytl[...], qcat[:, :128])

        @pl.loop(0, 8)
        def _(i):
            a = pl.ds(pl.multiple_of(i * 64, 64), 64)
            b = pl.ds(pl.multiple_of(i * 64 + 512, 64), 64)
            dy = res[a, :128] + res[a, 128:] + res2[a]
            dyy = res[b, :128] + res[b, 128:] + res2[b]
            t_ab[pair, a] = nu_lane * dyy - vv[a] * dy

    for i in range(7):
        forward(0, i).wait_recv()
    start = r_ab[0]
    lo_all = lax.broadcasted_iota(jnp.int32, (512, 128), 1) < 64
    vv[...] = STEP * jnp.where(lo_all, start, pltpu.roll(start, 64, 1))
    y_pair(0, nu[1], nu[0])
    answer(0, 30)
    for i in range(7):
        backward(0, i).start()
    b_ab[0, line] = t_ab[0, here]

    for i in range(7):
        forward(1, i).wait_recv()
    y_pair(1, nu[2], nu[3])
    answer(30, 60)
    for i in range(7):
        backward(1, i).start()
    b_ab[1, line] = t_ab[1, here]

    for i in range(7):
        forward(2, i).wait_recv()
    for s in range(8):
        part = r_c[s]
        turned = pltpu.roll(part, 64, 1)
        for half, (keep, other) in enumerate(((part, turned), (turned, part))):
            high = keep.astype(BF16).astype(F32)
            low = other - other.astype(BF16).astype(F32)
            rows = slice(64 * s + 32 * half, 64 * s + 32 * half + 32)
            qcat[rows, :128] = jnp.where(lo32, high, low).astype(BF16)
    res2[...] = mm(yth[...], qcat[:, :128]) + mm(ytl[...], qcat[:, :128])

    @pl.loop(0, 8)
    def _(i):
        a = pl.ds(pl.multiple_of(i * 64, 64), 64)
        b = pl.ds(pl.multiple_of(i * 64 + 512, 64), 64)
        dy = res2[a] + pltpu.roll(res2[a], 64, 1)
        dyy = res2[b] + pltpu.roll(res2[b], 64, 1)
        term = (STEP * nu[4]) * dyy - vv[a] * dy
        t_c[i] = jnp.where(lo32, term[:32], term[32:])

    for i in range(7):
        backward(2, i).start()
    b_c[line] = t_c[line]

    loads[8].wait()

    @pl.loop(0, 8)
    def _(i):
        rows = pl.ds(pl.multiple_of(i * 64, 64), 64)
        high, low = split(xop[rows])
        xh[rows] = high
        xl[rows] = low

    for v in range(5):
        high, low = split(m[v])
        mh[64 * v : 64 * v + 64] = high
        ml[64 * v : 64 * v + 64] = low
    for n in range(2):
        deriv = []
        for o in range(2):
            cols = slice(512 * o + 256 * n, 512 * o + 256 * n + 256)
            deriv.append(
                mm(mh[...], xh[:, cols])
                + mm(ml[...], xh[:, cols])
                + mm(mh[...], xl[:, cols])
            )
        cols = slice(256 * n, 256 * n + 256)
        u = STEP * m[0, :, cols]
        for v in range(5):
            rows = slice(64 * v, 64 * v + 64)
            term = m[v, :, cols] + (STEP * nu[v]) * deriv[1][rows] - u * deriv[0][rows]
            if v == 1:
                term = term + (STEP * coef[5]) * m[3, :, cols] + (STEP * coef[6]) * m[4, :, cols]
            acc[v, :, cols] = term

    ghost_stage()

    for pair, (first, second) in enumerate(((1, 0), (2, 3))):
        for i in range(7):
            backward(pair, i).wait_recv()
        for c in range(4):
            cols = slice(128 * c, 128 * c + 128)
            a, b = b_ab[pair, 2 * c], b_ab[pair, 2 * c + 1]
            acc[first, :, cols] += jnp.where(lo, a, pltpu.roll(b, 64, 1))
            acc[second, :, cols] += jnp.where(lo, pltpu.roll(a, 64, 1), b)

    @pl.loop(0, ny)
    def _(yy):
        @pl.when(yy != y)
        def _():
            y_copy(yy, yy).wait_recv()

    ghost = ry[0]
    for p in range(1, ny):
        ghost = ghost + ry[p]
    one, two = ghost[:, :128], ghost[:, 128:]
    row = plane_row[:, :128]
    last = jnp.where(row < 2, pltpu.roll(one, 2, 0), pltpu.roll(two, 4, 0))
    last = jnp.where((row == 3) | (row == 4), pltpu.roll(pltpu.roll(one, 64, 1), 5, 0), last)
    last = jnp.where(row == 5, pltpu.roll(pltpu.roll(two, 64, 1), 7, 0), last)
    ghost = jnp.concatenate([one, two, jnp.where(lanes[:8] < 64, last, 0.0)], axis=1)
    flip = jnp.where(plane_row < 3, 1.0 - own[0], own[1])
    turned = jnp.where(
        (plane_row == 0) | (plane_row == 3),
        pltpu.roll(ghost, 6, 0),
        jnp.where((plane_row == 2) | (plane_row == 5), pltpu.roll(ghost, 2, 0), ghost),
    )
    column = lax.broadcasted_iota(jnp.int32, (8, 384), 1)
    turned = jnp.where(column < 64, -turned, turned)
    ghost = jnp.where(flip > 0.5, turned, ghost)
    ghost = jnp.where(plane_row < 6, ghost, 0.0)
    ghost_high = ghost.astype(BF16).astype(F32)
    stack = jnp.concatenate([ghost_high, ghost - ghost_high, ghost_high, jnp.zeros((104, 384), F32)], axis=0)
    ghost_t = jnp.concatenate(
        [jnp.transpose(stack[:, 128 * j : 128 * j + 128]) for j in range(3)], axis=0
    )[:320].astype(BF16)
    for n in range(2):
        cols = slice(256 * n, 256 * n + 256)
        dx = mm(ghost_t, gstack[:, cols])
        dxx = mm(ghost_t, gstack[:, 256 * n + 512 : 256 * n + 768])
        u = STEP * m[0, :, cols]
        for v in range(5):
            rows = slice(64 * v, 64 * v + 64)
            term = acc[v, :, cols] + (STEP * nu[v]) * dxx[rows] - u * dx[rows]
            if v < 4:
                out[v, :, cols] = jnp.concatenate([live, live], axis=1) * term
            else:
                acc[v, :, cols] = term

    for i in range(7):
        backward(2, i).wait_recv()
    for c in range(4):
        cols = slice(128 * c, 128 * c + 128)
        a, b = b_c[2 * c], b_c[2 * c + 1]
        top = jnp.where(lo32, a, pltpu.roll(b, 64, 1))
        bottom = jnp.where(lo32, pltpu.roll(a, 64, 1), b)
        out[4, :32, cols] = live[:32] * (acc[4, :32, cols] + top)
        out[4, 32:, cols] = live[32:] * (acc[4, 32:, cols] + bottom)

    for chunk in range(3):
        for i in range(7):
            forward(chunk, i).wait_send()
            backward(chunk, i).wait_send()

    @pl.loop(0, nz)
    def _(zz):
        @pl.when(zz != z)
        def _():
            z_copy(zz, z).wait_send()

    @pl.loop(0, ny)
    def _(yy):
        @pl.when(yy != y)
        def _():
            y_copy(yy, y).wait_send()


def on_device(
    nz,
    ny,
    flow_state,
    block_owner,
    link_block,
    link_side,
    rows_live,
    x_operator,
    ghost_operator,
    y_operator,
    coefficients,
):
    any_spec = pl.BlockSpec(memory_space=pltpu.HBM)
    dma = pltpu.SemaphoreType.DMA
    blocks = nz * ny
    result = pl.pallas_call(
        functools.partial(kernel, nz, ny, 111 if nz > 8 else 15 * nz + 3),
        out_shape=jax.ShapeDtypeStruct((5, 64, 512), F32),
        in_specs=[any_spec] * 9,
        out_specs=pl.BlockSpec(memory_space=pltpu.VMEM),
        scratch_shapes=[
            pltpu.VMEM((5, 64, 512), F32),
            pltpu.VMEM((1, blocks), jnp.int32),
            pltpu.VMEM((2, blocks), jnp.int32),
            pltpu.VMEM((2, blocks), jnp.int32),
            pltpu.VMEM((1, blocks), jnp.int32),
            pltpu.SMEM((7,), F32),
            pltpu.VMEM((6, 1024), F32),
            pltpu.VMEM((512, 1024), F32),
            pltpu.VMEM((512, 1024), F32),
            pltpu.VMEM((512, 1024), BF16),
            pltpu.VMEM((512, 1024), BF16),
            pltpu.VMEM((1024, 512), BF16),
            pltpu.VMEM((1024, 512), BF16),
            pltpu.VMEM((320, 512), BF16),
            pltpu.VMEM((320, 512), BF16),
            pltpu.VMEM((2, 8, 64, 128), F32),
            pltpu.VMEM((8, 32, 128), F32),
            pltpu.VMEM((2, 512, 128), F32),
            pltpu.VMEM((8, 32, 128), F32),
            pltpu.VMEM((2, 512, 128), F32),
            pltpu.VMEM((8, 32, 128), F32),
            pltpu.VMEM((2, 8, 64, 128), F32),
            pltpu.VMEM((8, 32, 128), F32),
            pltpu.VMEM((512, 128), F32),
            pltpu.VMEM((512, 256), BF16),
            pltpu.VMEM((1024, 256), F32),
            pltpu.VMEM((1024, 128), F32),
            pltpu.VMEM((5, 64, 512), F32),
            pltpu.VMEM((8, 256), F32),
            pltpu.VMEM((nz, 8, 256), F32),
            pltpu.VMEM((ny, 8, 256), F32),
            pltpu.VMEM((ny, 8, 256), F32),
            dma((9,)),
            dma((3, 7)),
            dma((3, 7)),
            dma((3, 7)),
            dma((3, 7)),
            dma((nz,)),
            dma((nz,)),
            dma((ny,)),
            dma((ny,)),
            pltpu.SemaphoreType.REGULAR,
            pltpu.VMEM((128, 1024), BF16),
        ],
        compiler_params=pltpu.CompilerParams(
            collective_id=0, has_side_effects=True, vmem_limit_bytes=40 * 1024 * 1024
        ),
        cost_estimate=pl.CostEstimate(flops=2 * 10**9, bytes_accessed=6 * 10**6, transcendentals=0),
    )(
        *(
            pltpu.with_memory_space_constraint(value, pltpu.HBM)
            for value in (
                flow_state[0],
                block_owner[None],
                link_block.T,
                link_side.T,
                rows_live[None],
                x_operator,
                ghost_operator,
                y_operator,
                coefficients,
            )
        )
    )
    return result[None]


def solution(mesh):
    blocks = mesh.shape["blk"]
    ny = min(NY, blocks // 2)
    return jax.shard_map(
        functools.partial(on_device, blocks // ny, ny),
        mesh=mesh,
        in_specs=(P("blk", None, "line", None), P(), P(), P(), P(), P(), P(), P(), P()),
        out_specs=P("blk", None, "line", None),
        check_vma=False,
    )
```

```python
import functools

import jax
import jax.numpy as jnp
from jax import lax
from jax.experimental import pallas as pl
from jax.experimental.pallas import tpu as pltpu
from jax.sharding import PartitionSpec as P

NY = 8
STEP = 0.3
MESH = pl.DeviceIdType.MESH
F32 = jnp.float32
BF16 = jnp.bfloat16
PEERS = ((1, 0), (3, 0), (1, 1), (3, 1), (2, 0), (2, 1), (0, 1))


def split(value):
    high = value.astype(BF16)
    return high, (value - high.astype(F32)).astype(BF16)


def mm(a, b):
    return jnp.dot(a, b, preferred_element_type=F32)


def kernel(
    nz,
    ny,
    z_late,
    flow,
    owner_h,
    link_block_h,
    link_side_h,
    rows_live_h,
    xop_h,
    gop_h,
    yop_h,
    coef_h,
    out,
    m,
    owner_v,
    link_block_v,
    link_side_v,
    rows_live_v,
    coef,
    gop,
    xop,
    yop,
    xh,
    xl,
    yth,
    ytl,
    mh,
    ml,
    s_ab,
    s_c,
    r_ab,
    r_c,
    t_ab,
    t_c,
    b_ab,
    b_c,
    vv,
    qcat,
    res,
    res2,
    acc,
    face,
    gz,
    sy,
    ry,
    load_sem,
    fs,
    fr,
    bs,
    br,
    zs,
    zr,
    ys,
    yr,
    ready,
    gstack,
):
    loads = [
        pltpu.make_async_copy(a, b, load_sem.at[i])
        for i, (a, b) in enumerate(
            (
                (rows_live_h, rows_live_v),
                (owner_h, owner_v),
                (flow, m),
                (link_block_h, link_block_v),
                (link_side_h, link_side_v),
                (coef_h, coef),
                (gop_h, gop),
                (yop_h, yop),
                (xop_h, xop),
            )
        )
    ]
    for load in loads:
        load.start()

    line = lax.axis_index("line")
    slot = lax.axis_index("blk")
    chip, core = line // 2, lax.rem(line, 2)
    z, y = slot // ny, lax.rem(slot, ny)

    def peer(ahead, other):
        return lax.rem(chip + ahead, 4) * 2 + lax.rem(core + other, 2)

    is_first = (slot == 0) & (line == 0)
    late_line = (slot == 0) & (line != 0)
    z_special = (y == 0) & (line == 0)
    y_special = (z == 0) & (line == 0) & (y != 0)

    def usual(zz):
        return jnp.where(zz < 8, 15 * zz, 88 + 4 * zz)

    my_z = jnp.where(is_first, z_late, usual(z))
    gaps = [jnp.where(z_special, z_late, 0) - my_z]
    gaps += [(15 * zz if zz < 8 else 88 + 4 * zz) - my_z for zz in range(1, nz)]
    close = [jnp.abs(gap) <= 10 for gap in gaps]
    close[0] = close[0] & jnp.logical_not(z_special)
    close = [here & jnp.logical_not(is_first) for here in close]
    now = [(z != zz) & ((gaps[zz] < 0) | close[zz]) for zz in range(nz)]

    barrier = pltpu.get_barrier_semaphore()

    @pl.when(jnp.logical_not(is_first))
    def _():
        for ahead, other in PEERS:
            pl.semaphore_signal(
                barrier, inc=1, device_id={"line": peer(ahead, other)}, device_id_type=MESH
            )

    waits = len(PEERS) - jnp.where(late_line, 1, 0) + ny - 1 - jnp.where(y_special, 1, 0)
    for zz in range(nz):
        waits += jnp.where(now[zz], 1, 0)

    for zz in range(nz):

        @pl.when((z != zz) & ((gaps[zz] > 0) | close[zz]))
        def _():
            pl.semaphore_signal(barrier, inc=1, device_id={"blk": zz * ny + y}, device_id_type=MESH)

    for yy in range(ny):

        @pl.when((y != yy) & jnp.logical_not(is_first))
        def _():
            pl.semaphore_signal(barrier, inc=1, device_id={"blk": z * ny + yy}, device_id_type=MESH)

    @pl.when(is_first)
    def _():
        pl.semaphore_wait(barrier, waits)
        for ahead, other in PEERS:
            pl.semaphore_signal(
                ready, inc=1, device_id={"line": peer(ahead, other)}, device_id_type=MESH
            )

        @pl.loop(1, ny)
        def _(yy):
            pl.semaphore_signal(ready, inc=1, device_id={"blk": z * ny + yy}, device_id_type=MESH)

    loads[0].wait()
    loads[1].wait()

    lanes = lax.broadcasted_iota(jnp.int32, (64, 128), 1)
    lo = lanes < 64
    mine = owner_v[...] == slot
    live_rows = jnp.sum(jnp.where(mine, rows_live_v[...].astype(F32), 0.0), axis=1, keepdims=True)
    row_id = (lax.broadcasted_iota(jnp.int32, (64, 128), 0) + line * 64).astype(F32)
    live = (row_id < live_rows).astype(F32)
    loads[2].wait()

    for pair, (first, second) in enumerate(((1, 0), (2, 3))):
        for c in range(4):
            cols = slice(128 * c, 128 * c + 128)
            a = m[first, :, cols] * live
            b = m[second, :, cols] * live
            m[first, :, cols] = a
            m[second, :, cols] = b
            s_ab[pair, 2 * c] = jnp.where(lo, a, pltpu.roll(b, 64, 1))
            s_ab[pair, 2 * c + 1] = jnp.where(lo, pltpu.roll(a, 64, 1), b)
    lo32 = lo[:32]
    for c in range(4):
        cols = slice(128 * c, 128 * c + 128)
        a = m[4, :, cols] * live
        m[4, :, cols] = a
        s_c[2 * c] = jnp.where(lo32, a[:32], pltpu.roll(a[32:], 64, 1))
        s_c[2 * c + 1] = jnp.where(lo32, pltpu.roll(a[:32], 64, 1), a[32:])

    planes = []
    for v in range(5):
        planes.append(jnp.where(lanes < 3, m[v, :, 0:128], pltpu.roll(m[v, :, 384:512], 6, 1)))
    last = planes[4]
    for v, moves in enumerate(((6, 6), (3, 3), (4, None), (1, None))):
        for lane, move in zip((6, 7), moves):
            if move is not None:
                planes[v] = jnp.where(lanes == lane, pltpu.roll(last, move, 1), planes[v])
    for j in range(2):
        both = jnp.concatenate([planes[2 * j], planes[2 * j + 1]], axis=0)
        face[:, 128 * j : 128 * j + 128] = jnp.transpose(both)[:8]

    @pl.when(jnp.logical_not(is_first))
    def _():
        pl.semaphore_wait(barrier, waits)

    here = pl.ds(pl.multiple_of(line * 64, 64), 64)

    def forward(chunk, i):
        ahead, other = PEERS[i]
        to = peer(ahead, other)
        if chunk < 2:
            source, target = s_ab.at[chunk, to], r_ab.at[chunk, here]
        else:
            source, target = s_c.at[to], r_c.at[line]
        return pltpu.make_async_remote_copy(
            src_ref=source,
            dst_ref=target,
            send_sem=fs.at[chunk, i],
            recv_sem=fr.at[chunk, i],
            device_id={"line": to},
            device_id_type=MESH,
        )

    def backward(chunk, i):
        ahead, other = PEERS[i]
        to = peer(ahead, other)
        if chunk < 2:
            source = t_ab.at[chunk, pl.ds(pl.multiple_of(to * 64, 64), 64)]
            target = b_ab.at[chunk, line]
        else:
            source, target = t_c.at[to], b_c.at[line]
        return pltpu.make_async_remote_copy(
            src_ref=source,
            dst_ref=target,
            send_sem=bs.at[chunk, i],
            recv_sem=br.at[chunk, i],
            device_id={"line": to},
            device_id_type=MESH,
        )

    def z_copy(zz, sender):
        return pltpu.make_async_remote_copy(
            src_ref=face,
            dst_ref=gz.at[sender],
            send_sem=zs.at[zz],
            recv_sem=zr.at[sender],
            device_id={"blk": zz * ny + y},
            device_id_type=MESH,
        )

    def y_copy(yy, sender):
        return pltpu.make_async_remote_copy(
            src_ref=sy.at[yy],
            dst_ref=ry.at[sender],
            send_sem=ys.at[yy],
            recv_sem=yr.at[sender],
            device_id={"blk": z * ny + yy},
            device_id_type=MESH,
        )

    def is_late(i):
        return late_line & (peer(*PEERS[i]) == 0)

    def send_forward(chunk, i):
        @pl.when(jnp.logical_not(is_late(i)))
        def _():
            forward(chunk, i).start()

    @pl.when(is_first)
    def _():
        for i in range(7):
            forward(0, i).start()

    for zz in range(nz):

        @pl.when(now[zz])
        def _():
            z_copy(zz, z).start()

    for i in range(7):

        @pl.when(jnp.logical_not(is_first | is_late(i)))
        def _():
            forward(0, i).start()

    for chunk in (1, 2):
        for i in range(7):
            send_forward(chunk, i)

    gz[z] = face[...]
    r_ab[0, here] = s_ab[0, line]
    r_ab[1, here] = s_ab[1, line]
    r_c[line] = s_c[line]

    loads[7].wait()

    @pl.loop(0, 8)
    def _(i):
        rows = pl.ds(pl.multiple_of(i * 128, 128), 128)
        for j in range(4):
            block = jnp.transpose(yop[128 * j : 128 * j + 128, rows])
            high, low = split(block)
            yth[rows, 128 * j : 128 * j + 128] = high
            ytl[rows, 128 * j : 128 * j + 128] = low

    loads[3].wait()
    loads[4].wait()
    peers_row = lax.broadcasted_iota(jnp.int32, (ny, nz * ny), 0) + z * ny
    lane_row = lax.broadcasted_iota(jnp.int32, (ny, nz * ny), 1).astype(F32)
    owner = owner_v[...]
    owner_f = owner.astype(F32)
    hot = owner == peers_row
    wanted = []
    for side in range(2):
        partner = jnp.sum(
            jnp.where(hot, link_block_v[side : side + 1, :].astype(F32), 0.0), axis=1, keepdims=True
        )
        far = jnp.sum(
            jnp.where(hot, link_side_v[side : side + 1, :].astype(F32), 0.0), axis=1, keepdims=True
        )
        source = jnp.sum(jnp.where(lane_row == partner, owner_f, 0.0), axis=1, keepdims=True)
        source = source.astype(jnp.int32)
        source_z = source // ny
        bits = []
        while 2 ** len(bits) < nz:
            bits.append((source_z // 2 ** len(bits) % 2).astype(F32))
        wanted.append((bits, far, (source % ny == y).astype(F32)))

    own = []
    for side in range(2):
        own.append(
            jnp.sum(jnp.where(mine, link_side_v[side : side + 1, :].astype(F32), 0.0), axis=1, keepdims=True)
        )

    loads[6].wait()
    g_op = jnp.concatenate([gop[...], jnp.zeros((2, 1024), F32)], axis=0)
    g_high = g_op.astype(BF16).astype(F32)
    gstack[...] = jnp.concatenate(
        [g_high, g_high, g_op - g_high, jnp.zeros((104, 1024), F32)], axis=0
    ).astype(BF16)

    plane_row = lax.broadcasted_iota(jnp.int32, (8, 384), 0)
    wide_row = plane_row[:, :256]
    half = lax.rem(lax.broadcasted_iota(jnp.int32, (8, 256), 1), 128) // 64
    of_face = [
        ((wide_row >= 3 * f) & (wide_row < 3 * f + 3)) | ((wide_row >= 6) & (half == f))
        for f in range(2)
    ]

    def between(zz, least, most):
        return (gaps[zz] > least) & (gaps[zz] <= most) & jnp.logical_not(close[zz])

    order = (*range(1, min(8, nz)), 0, *range(8, nz))

    def answer(least, most, first_most=None):
        for zz in order:

            @pl.when(between(zz, least, most if zz or first_most is None else first_most))
            def _():
                z_copy(zz, zz).wait_recv()
                z_copy(zz, z).start()

    def ghost_stage():
        for zz in range(1, nz):

            @pl.when(between(zz, 45, 1000))
            def _():
                z_copy(zz, zz).wait_recv()

            @pl.when(between(zz, 45, 80))
            def _():
                z_copy(zz, z).start()

        for zz in range(nz):

            @pl.when(now[zz])
            def _():
                z_copy(zz, zz).wait_recv()

        for p in range(ny):
            message = jnp.zeros((8, 256), F32)
            for side in range(2):
                far = jnp.broadcast_to(wanted[side][1][p : p + 1], (8, 256))
                level = [gz[zz] for zz in range(nz)]
                for bits in wanted[side][0]:
                    bit = jnp.broadcast_to(bits[p : p + 1], (8, 256)) > 0.5
                    level = [
                        jnp.where(bit, level[k + 1], level[k]) for k in range(0, len(level), 2)
                    ]
                inside = jnp.broadcast_to(wanted[side][2][p : p + 1], (8, 256)) > 0.5
                total = jnp.where(inside, level[0], 0.0)
                halves = jnp.concatenate(
                    [pltpu.roll(total[:, 128 * j : 128 * j + 128], 64, 1) for j in range(2)], axis=1
                )
                swapped = jnp.where(wide_row < 6, pltpu.roll(total, 3 if side else 5, 0), halves)
                chosen = jnp.where(jnp.abs(far - side) < 0.5, total, swapped)
                message = jnp.where(of_face[side], chosen, message)
            sy[p] = message

        @pl.when(y_special)
        def _():
            pl.semaphore_wait(ready, 1)

        for yy in range(ny):

            @pl.when(y != yy)
            def _():
                y_copy(yy, y).start()

        for zz in range(1, nz):

            @pl.when(between(zz, 80, 1000))
            def _():
                z_copy(zz, z).start()

        ry[y] = sy[y]

    @pl.when(late_line)
    def _():
        pl.semaphore_wait(ready, 1)

    for chunk in range(3):
        for i in range(7):

            @pl.when(is_late(i))
            def _():
                forward(chunk, i).start()

    loads[5].wait()
    nu = [coef[v] for v in range(5)]

    def y_pair(pair, nu_first, nu_second):
        nu_lane = STEP * jnp.where(lo, nu_first, nu_second)
        high, low = split(r_ab[pair])
        qcat[:, :128] = high
        qcat[:, 128:] = low
        res[...] = mm(yth[...], qcat[...])
        res2[...] = mm(ytl[...], qcat[:, :128])

        @pl.loop(0, 8)
        def _(i):
            a = pl.ds(pl.multiple_of(i * 64, 64), 64)
            b = pl.ds(pl.multiple_of(i * 64 + 512, 64), 64)
            dy = res[a, :128] + res[a, 128:] + res2[a]
            dyy = res[b, :128] + res[b, 128:] + res2[b]
            t_ab[pair, a] = nu_lane * dyy - vv[a] * dy

    for i in range(7):
        forward(0, i).wait_recv()
    start = r_ab[0]
    lo_all = lax.broadcasted_iota(jnp.int32, (512, 128), 1) < 64
    vv[...] = STEP * jnp.where(lo_all, start, pltpu.roll(start, 64, 1))
    y_pair(0, nu[1], nu[0])
    answer(0, 20, 20)
    for i in range(7):
        backward(0, i).start()
    b_ab[0, line] = t_ab[0, here]

    for i in range(7):
        forward(1, i).wait_recv()
    y_pair(1, nu[2], nu[3])
    answer(20, 45, 1000)
    for i in range(7):
        backward(1, i).start()
    b_ab[1, line] = t_ab[1, here]

    for i in range(7):
        forward(2, i).wait_recv()
    for s in range(8):
        part = r_c[s]
        turned = pltpu.roll(part, 64, 1)
        for half, (keep, other) in enumerate(((part, turned), (turned, part))):
            high = keep.astype(BF16).astype(F32)
            low = other - other.astype(BF16).astype(F32)
            rows = slice(64 * s + 32 * half, 64 * s + 32 * half + 32)
            qcat[rows, :128] = jnp.where(lo32, high, low).astype(BF16)
    res2[...] = mm(yth[...], qcat[:, :128]) + mm(ytl[...], qcat[:, :128])

    @pl.loop(0, 8)
    def _(i):
        a = pl.ds(pl.multiple_of(i * 64, 64), 64)
        b = pl.ds(pl.multiple_of(i * 64 + 512, 64), 64)
        dy = res2[a] + pltpu.roll(res2[a], 64, 1)
        dyy = res2[b] + pltpu.roll(res2[b], 64, 1)
        term = (STEP * nu[4]) * dyy - vv[a] * dy
        t_c[i] = jnp.where(lo32, term[:32], term[32:])

    for i in range(7):
        backward(2, i).start()
    b_c[line] = t_c[line]
    pl.when(is_first)(ghost_stage)

    loads[8].wait()

    @pl.loop(0, 8)
    def _(i):
        rows = pl.ds(pl.multiple_of(i * 64, 64), 64)
        high, low = split(xop[rows])
        xh[rows] = high
        xl[rows] = low

    for v in range(5):
        high, low = split(m[v])
        mh[64 * v : 64 * v + 64] = high
        ml[64 * v : 64 * v + 64] = low
    for n in range(2):
        deriv = []
        for o in range(2):
            cols = slice(512 * o + 256 * n, 512 * o + 256 * n + 256)
            deriv.append(
                mm(mh[...], xh[:, cols])
                + mm(ml[...], xh[:, cols])
                + mm(mh[...], xl[:, cols])
            )
        cols = slice(256 * n, 256 * n + 256)
        u = STEP * m[0, :, cols]
        for v in range(5):
            rows = slice(64 * v, 64 * v + 64)
            term = m[v, :, cols] + (STEP * nu[v]) * deriv[1][rows] - u * deriv[0][rows]
            if v == 1:
                term = term + (STEP * coef[5]) * m[3, :, cols] + (STEP * coef[6]) * m[4, :, cols]
            acc[v, :, cols] = term

    pl.when(jnp.logical_not(is_first))(ghost_stage)

    for pair, (first, second) in enumerate(((1, 0), (2, 3))):
        for i in range(7):
            backward(pair, i).wait_recv()
        for c in range(4):
            cols = slice(128 * c, 128 * c + 128)
            a, b = b_ab[pair, 2 * c], b_ab[pair, 2 * c + 1]
            acc[first, :, cols] += jnp.where(lo, a, pltpu.roll(b, 64, 1))
            acc[second, :, cols] += jnp.where(lo, pltpu.roll(a, 64, 1), b)

    for chunk in range(3):
        for i in range(7):
            forward(chunk, i).wait_send()
            if chunk < 2:
                backward(chunk, i).wait_send()
    for zz in range(nz):

        @pl.when(z != zz)
        def _():
            z_copy(zz, z).wait_send()

    for yy in range(ny):

        @pl.when(y != yy)
        def _():
            y_copy(yy, yy).wait_recv()

    for yy in range(ny):

        @pl.when(y != yy)
        def _():
            y_copy(yy, y).wait_send()

    ghost = ry[0]
    for p in range(1, ny):
        ghost = ghost + ry[p]
    one, two = ghost[:, :128], ghost[:, 128:]
    row = plane_row[:, :128]
    last = jnp.where(row < 2, pltpu.roll(one, 2, 0), pltpu.roll(two, 4, 0))
    last = jnp.where((row == 3) | (row == 4), pltpu.roll(pltpu.roll(one, 64, 1), 5, 0), last)
    last = jnp.where(row == 5, pltpu.roll(pltpu.roll(two, 64, 1), 7, 0), last)
    ghost = jnp.concatenate([one, two, jnp.where(lanes[:8] < 64, last, 0.0)], axis=1)
    flip = jnp.where(plane_row < 3, 1.0 - own[0], own[1])
    turned = jnp.where(
        (plane_row == 0) | (plane_row == 3),
        pltpu.roll(ghost, 6, 0),
        jnp.where((plane_row == 2) | (plane_row == 5), pltpu.roll(ghost, 2, 0), ghost),
    )
    column = lax.broadcasted_iota(jnp.int32, (8, 384), 1)
    turned = jnp.where(column < 64, -turned, turned)
    ghost = jnp.where(flip > 0.5, turned, ghost)
    ghost = jnp.where(plane_row < 6, ghost, 0.0)
    ghost_high = ghost.astype(BF16).astype(F32)
    stack = jnp.concatenate([ghost_high, ghost - ghost_high, ghost_high, jnp.zeros((104, 384), F32)], axis=0)
    ghost_t = jnp.concatenate(
        [jnp.transpose(stack[:, 128 * j : 128 * j + 128]) for j in range(3)], axis=0
    )[:320].astype(BF16)
    for n in range(2):
        cols = slice(256 * n, 256 * n + 256)
        dx = mm(ghost_t, gstack[:, cols])
        dxx = mm(ghost_t, gstack[:, 256 * n + 512 : 256 * n + 768])
        u = STEP * m[0, :, cols]
        for v in range(5):
            rows = slice(64 * v, 64 * v + 64)
            term = acc[v, :, cols] + (STEP * nu[v]) * dxx[rows] - u * dx[rows]
            if v < 4:
                out[v, :, cols] = jnp.concatenate([live, live], axis=1) * term
            else:
                acc[v, :, cols] = term

    for i in range(7):
        backward(2, i).wait_recv()
    for c in range(4):
        cols = slice(128 * c, 128 * c + 128)
        a, b = b_c[2 * c], b_c[2 * c + 1]
        top = jnp.where(lo32, a, pltpu.roll(b, 64, 1))
        bottom = jnp.where(lo32, pltpu.roll(a, 64, 1), b)
        out[4, :32, cols] = live[:32] * (acc[4, :32, cols] + top)
        out[4, 32:, cols] = live[32:] * (acc[4, 32:, cols] + bottom)

    for i in range(7):
        backward(2, i).wait_send()


def on_device(
    nz,
    ny,
    flow_state,
    block_owner,
    link_block,
    link_side,
    rows_live,
    x_operator,
    ghost_operator,
    y_operator,
    coefficients,
):
    any_spec = pl.BlockSpec(memory_space=pltpu.HBM)
    dma = pltpu.SemaphoreType.DMA
    blocks = nz * ny
    result = pl.pallas_call(
        functools.partial(kernel, nz, ny, 111 if nz > 8 else 15 * nz + 3),
        out_shape=jax.ShapeDtypeStruct((5, 64, 512), F32),
        in_specs=[any_spec] * 9,
        out_specs=pl.BlockSpec(memory_space=pltpu.VMEM),
        scratch_shapes=[
            pltpu.VMEM((5, 64, 512), F32),
            pltpu.VMEM((1, blocks), jnp.int32),
            pltpu.VMEM((2, blocks), jnp.int32),
            pltpu.VMEM((2, blocks), jnp.int32),
            pltpu.VMEM((1, blocks), jnp.int32),
            pltpu.SMEM((7,), F32),
            pltpu.VMEM((6, 1024), F32),
            pltpu.VMEM((512, 1024), F32),
            pltpu.VMEM((512, 1024), F32),
            pltpu.VMEM((512, 1024), BF16),
            pltpu.VMEM((512, 1024), BF16),
            pltpu.VMEM((1024, 512), BF16),
            pltpu.VMEM((1024, 512), BF16),
            pltpu.VMEM((320, 512), BF16),
            pltpu.VMEM((320, 512), BF16),
            pltpu.VMEM((2, 8, 64, 128), F32),
            pltpu.VMEM((8, 32, 128), F32),
            pltpu.VMEM((2, 512, 128), F32),
            pltpu.VMEM((8, 32, 128), F32),
            pltpu.VMEM((2, 512, 128), F32),
            pltpu.VMEM((8, 32, 128), F32),
            pltpu.VMEM((2, 8, 64, 128), F32),
            pltpu.VMEM((8, 32, 128), F32),
            pltpu.VMEM((512, 128), F32),
            pltpu.VMEM((512, 256), BF16),
            pltpu.VMEM((1024, 256), F32),
            pltpu.VMEM((1024, 128), F32),
            pltpu.VMEM((5, 64, 512), F32),
            pltpu.VMEM((8, 256), F32),
            pltpu.VMEM((nz, 8, 256), F32),
            pltpu.VMEM((ny, 8, 256), F32),
            pltpu.VMEM((ny, 8, 256), F32),
            dma((9,)),
            dma((3, 7)),
            dma((3, 7)),
            dma((3, 7)),
            dma((3, 7)),
            dma((nz,)),
            dma((nz,)),
            dma((ny,)),
            dma((ny,)),
            pltpu.SemaphoreType.REGULAR,
            pltpu.VMEM((128, 1024), BF16),
        ],
        compiler_params=pltpu.CompilerParams(
            collective_id=0, has_side_effects=True, vmem_limit_bytes=40 * 1024 * 1024
        ),
        cost_estimate=pl.CostEstimate(flops=2 * 10**9, bytes_accessed=6 * 10**6, transcendentals=0),
    )(
        *(
            pltpu.with_memory_space_constraint(value, pltpu.HBM)
            for value in (
                flow_state[0],
                block_owner[None],
                link_block.T,
                link_side.T,
                rows_live[None],
                x_operator,
                ghost_operator,
                y_operator,
                coefficients,
            )
        )
    )
    return result[None]


def solution(mesh):
    blocks = mesh.shape["blk"]
    ny = min(NY, blocks // 2)
    return jax.shard_map(
        functools.partial(on_device, blocks // ny, ny),
        mesh=mesh,
        in_specs=(P("blk", None, "line", None), P(), P(), P(), P(), P(), P(), P(), P()),
        out_specs=P("blk", None, "line", None),
        check_vma=False,
    )
```

```python
import functools

import jax
import jax.numpy as jnp
from jax import lax
from jax.experimental import pallas as pl
from jax.experimental.pallas import tpu as pltpu
from jax.sharding import PartitionSpec as P

NY = 8
STEP = 0.3
MESH = pl.DeviceIdType.MESH
F32 = jnp.float32
BF16 = jnp.bfloat16
PEERS = ((1, 0), (3, 0), (1, 1), (3, 1), (2, 0), (2, 1), (0, 1))


def split(value):
    high = value.astype(BF16)
    return high, (value - high.astype(F32)).astype(BF16)


def mm(a, b):
    return jnp.dot(a, b, preferred_element_type=F32)


def kernel(
    nz,
    ny,
    z_late,
    flow,
    owner_h,
    link_block_h,
    link_side_h,
    rows_live_h,
    xop_h,
    gop_h,
    yop_h,
    coef_h,
    out,
    m,
    owner_v,
    link_block_v,
    link_side_v,
    rows_live_v,
    coef,
    gop,
    xop,
    yop,
    xh,
    xl,
    yth,
    ytl,
    mh,
    ml,
    s_ab,
    s_c,
    r_ab,
    r_c,
    t_ab,
    t_c,
    b_ab,
    b_c,
    vv,
    qcat,
    res,
    res2,
    acc,
    face,
    gz,
    sy,
    ry,
    load_sem,
    fs,
    fr,
    bs,
    br,
    zs,
    zr,
    ys,
    yr,
    ready,
    gstack,
):
    loads = [
        pltpu.make_async_copy(a, b, load_sem.at[i])
        for i, (a, b) in enumerate(
            (
                (rows_live_h, rows_live_v),
                (owner_h, owner_v),
                (flow, m),
                (link_block_h, link_block_v),
                (link_side_h, link_side_v),
                (coef_h, coef),
                (gop_h, gop),
                (yop_h, yop),
                (xop_h, xop),
            )
        )
    ]
    for load in loads:
        load.start()

    line = lax.axis_index("line")
    slot = lax.axis_index("blk")
    chip, core = line // 2, lax.rem(line, 2)
    z, y = slot // ny, lax.rem(slot, ny)

    def peer(ahead, other):
        return lax.rem(chip + ahead, 4) * 2 + lax.rem(core + other, 2)

    is_first = (slot == 0) & (line == 0)
    late_line = (slot == 0) & (line != 0)
    z_special = (y == 0) & (line == 0)
    y_special = (z == 0) & (line == 0) & (y != 0)

    def usual(zz):
        return jnp.where(zz < 8, 15 * zz, 88 + 4 * zz)

    my_z = jnp.where(is_first, z_late, usual(z))
    gaps = [jnp.where(z_special, z_late, 0) - my_z]
    gaps += [(15 * zz if zz < 8 else 88 + 4 * zz) - my_z for zz in range(1, nz)]
    close = [jnp.abs(gap) <= 10 for gap in gaps]
    close[0] = close[0] & jnp.logical_not(z_special)
    close = [here & jnp.logical_not(is_first) for here in close]
    now = [(z != zz) & ((gaps[zz] < 0) | close[zz]) for zz in range(nz)]

    barrier = pltpu.get_barrier_semaphore()

    @pl.when(jnp.logical_not(is_first))
    def _():
        for ahead, other in PEERS:
            pl.semaphore_signal(
                barrier, inc=1, device_id={"line": peer(ahead, other)}, device_id_type=MESH
            )

    waits = len(PEERS) - jnp.where(late_line, 1, 0) + ny - 1 - jnp.where(y_special, 1, 0)
    for zz in range(nz):
        waits += jnp.where(now[zz], 1, 0)

    for zz in range(nz):

        @pl.when((z != zz) & ((gaps[zz] > 0) | close[zz]))
        def _():
            pl.semaphore_signal(barrier, inc=1, device_id={"blk": zz * ny + y}, device_id_type=MESH)

    for yy in range(ny):

        @pl.when((y != yy) & jnp.logical_not(is_first))
        def _():
            pl.semaphore_signal(barrier, inc=1, device_id={"blk": z * ny + yy}, device_id_type=MESH)

    @pl.when(is_first)
    def _():
        pl.semaphore_wait(barrier, waits)
        for ahead, other in PEERS:
            pl.semaphore_signal(
                ready, inc=1, device_id={"line": peer(ahead, other)}, device_id_type=MESH
            )

        @pl.loop(1, ny)
        def _(yy):
            pl.semaphore_signal(ready, inc=1, device_id={"blk": z * ny + yy}, device_id_type=MESH)

    loads[0].wait()
    loads[1].wait()

    lanes = lax.broadcasted_iota(jnp.int32, (64, 128), 1)
    lo = lanes < 64
    mine = owner_v[...] == slot
    live_rows = jnp.sum(jnp.where(mine, rows_live_v[...].astype(F32), 0.0), axis=1, keepdims=True)
    row_id = (lax.broadcasted_iota(jnp.int32, (64, 128), 0) + line * 64).astype(F32)
    live = (row_id < live_rows).astype(F32)
    loads[2].wait()

    planes = []
    for v in range(5):
        low, high = m[v, :, 0:128], pltpu.roll(m[v, :, 384:512], 6, 1)
        planes.append(live * jnp.where(lanes < 3, low, high))
    last = planes[4]
    for v, moves in enumerate(((6, 6), (3, 3), (4, None), (1, None))):
        for lane, move in zip((6, 7), moves):
            if move is not None:
                planes[v] = jnp.where(lanes == lane, pltpu.roll(last, move, 1), planes[v])
    for j in range(2):
        both = jnp.concatenate([planes[2 * j], planes[2 * j + 1]], axis=0)
        face[:, 128 * j : 128 * j + 128] = jnp.transpose(both)[:8]

    @pl.when(jnp.logical_not(is_first))
    def _():
        pl.semaphore_wait(barrier, waits)

    here = pl.ds(pl.multiple_of(line * 64, 64), 64)

    def forward(chunk, i):
        ahead, other = PEERS[i]
        to = peer(ahead, other)
        if chunk < 2:
            source, target = s_ab.at[chunk, to], r_ab.at[chunk, here]
        else:
            source, target = s_c.at[to], r_c.at[line]
        return pltpu.make_async_remote_copy(
            src_ref=source,
            dst_ref=target,
            send_sem=fs.at[chunk, i],
            recv_sem=fr.at[chunk, i],
            device_id={"line": to},
            device_id_type=MESH,
        )

    def backward(chunk, i):
        ahead, other = PEERS[i]
        to = peer(ahead, other)
        if chunk < 2:
            source = t_ab.at[chunk, pl.ds(pl.multiple_of(to * 64, 64), 64)]
            target = b_ab.at[chunk, line]
        else:
            source, target = t_c.at[to], b_c.at[line]
        return pltpu.make_async_remote_copy(
            src_ref=source,
            dst_ref=target,
            send_sem=bs.at[chunk, i],
            recv_sem=br.at[chunk, i],
            device_id={"line": to},
            device_id_type=MESH,
        )

    def z_copy(zz, sender):
        return pltpu.make_async_remote_copy(
            src_ref=face,
            dst_ref=gz.at[sender],
            send_sem=zs.at[zz],
            recv_sem=zr.at[sender],
            device_id={"blk": zz * ny + y},
            device_id_type=MESH,
        )

    def y_copy(yy, sender):
        return pltpu.make_async_remote_copy(
            src_ref=sy.at[yy],
            dst_ref=ry.at[sender],
            send_sem=ys.at[yy],
            recv_sem=yr.at[sender],
            device_id={"blk": z * ny + yy},
            device_id_type=MESH,
        )

    def is_late(i):
        return late_line & (peer(*PEERS[i]) == 0)

    def send_forward(chunk, i):
        @pl.when(jnp.logical_not(is_late(i)))
        def _():
            forward(chunk, i).start()

    for zz in range(nz):

        @pl.when(now[zz] if zz < 8 else now[zz] & (z < 8))
        def _():
            z_copy(zz, z).start()

    def pack(pair, first, second):
        for c in range(4):
            cols = slice(128 * c, 128 * c + 128)
            a = m[first, :, cols] * live
            b = m[second, :, cols] * live
            m[first, :, cols] = a
            m[second, :, cols] = b
            s_ab[pair, 2 * c] = jnp.where(lo, a, pltpu.roll(b, 64, 1))
            s_ab[pair, 2 * c + 1] = jnp.where(lo, pltpu.roll(a, 64, 1), b)
    pack(0, 1, 0)
    for i in range(7):
        send_forward(0, i)
    pack(1, 2, 3)
    for i in range(7):
        send_forward(1, i)
    lo32 = lo[:32]
    for c in range(4):
        cols = slice(128 * c, 128 * c + 128)
        a = m[4, :, cols] * live
        m[4, :, cols] = a
        s_c[2 * c] = jnp.where(lo32, a[:32], pltpu.roll(a[32:], 64, 1))
        s_c[2 * c + 1] = jnp.where(lo32, pltpu.roll(a[:32], 64, 1), a[32:])

    for i in range(7):
        send_forward(2, i)
    for zz in range(8, nz):

        @pl.when(now[zz] & (z >= 8))
        def _():
            z_copy(zz, z).start()

    gz[z] = face[...]
    r_ab[0, here] = s_ab[0, line]
    r_ab[1, here] = s_ab[1, line]
    r_c[line] = s_c[line]

    loads[7].wait()

    @pl.loop(0, 8)
    def _(i):
        rows = pl.ds(pl.multiple_of(i * 128, 128), 128)
        for j in range(4):
            block = jnp.transpose(yop[128 * j : 128 * j + 128, rows])
            high, low = split(block)
            yth[rows, 128 * j : 128 * j + 128] = high
            ytl[rows, 128 * j : 128 * j + 128] = low

    loads[3].wait()
    loads[4].wait()
    peers_row = lax.broadcasted_iota(jnp.int32, (ny, nz * ny), 0) + z * ny
    lane_row = lax.broadcasted_iota(jnp.int32, (ny, nz * ny), 1).astype(F32)
    owner = owner_v[...]
    owner_f = owner.astype(F32)
    hot = owner == peers_row
    wanted = []
    for side in range(2):
        partner = jnp.sum(
            jnp.where(hot, link_block_v[side : side + 1, :].astype(F32), 0.0), axis=1, keepdims=True
        )
        far = jnp.sum(
            jnp.where(hot, link_side_v[side : side + 1, :].astype(F32), 0.0), axis=1, keepdims=True
        )
        source = jnp.sum(jnp.where(lane_row == partner, owner_f, 0.0), axis=1, keepdims=True)
        source = source.astype(jnp.int32)
        source_z = source // ny
        bits = []
        while 2 ** len(bits) < nz:
            bits.append((source_z // 2 ** len(bits) % 2).astype(F32))
        wanted.append((bits, far, (source % ny == y).astype(F32)))

    own = []
    for side in range(2):
        own.append(
            jnp.sum(jnp.where(mine, link_side_v[side : side + 1, :].astype(F32), 0.0), axis=1, keepdims=True)
        )

    loads[6].wait()
    g_op = jnp.concatenate([gop[...], jnp.zeros((2, 1024), F32)], axis=0)
    g_high = g_op.astype(BF16).astype(F32)
    gstack[...] = jnp.concatenate(
        [g_high, g_high, g_op - g_high, jnp.zeros((104, 1024), F32)], axis=0
    ).astype(BF16)

    plane_row = lax.broadcasted_iota(jnp.int32, (8, 384), 0)
    wide_row = plane_row[:, :256]
    half = lax.rem(lax.broadcasted_iota(jnp.int32, (8, 256), 1), 128) // 64
    of_face = [
        ((wide_row >= 3 * f) & (wide_row < 3 * f + 3)) | ((wide_row >= 6) & (half == f))
        for f in range(2)
    ]

    def between(zz, least, most):
        return (gaps[zz] > least) & (gaps[zz] <= most) & jnp.logical_not(close[zz])

    order = (*range(1, min(8, nz)), 0, *range(8, nz))

    def answer(least, most, first_least, first_most):
        for zz in order:

            @pl.when(between(zz, least, most) if zz else between(zz, first_least, first_most))
            def _():
                z_copy(zz, zz).wait_recv()
                z_copy(zz, z).start()

    def ghost_stage(least=45):
        for zz in range(1, nz):

            @pl.when(between(zz, least, 1000))
            def _():
                z_copy(zz, zz).wait_recv()

            @pl.when(between(zz, least, 80))
            def _():
                z_copy(zz, z).start()

        for zz in range(nz):

            @pl.when(now[zz])
            def _():
                z_copy(zz, zz).wait_recv()

        for p in range(ny):
            message = jnp.zeros((8, 256), F32)
            for side in range(2):
                far = jnp.broadcast_to(wanted[side][1][p : p + 1], (8, 256))
                level = [gz[zz] for zz in range(nz)]
                for bits in wanted[side][0]:
                    bit = jnp.broadcast_to(bits[p : p + 1], (8, 256)) > 0.5
                    level = [
                        jnp.where(bit, level[k + 1], level[k]) for k in range(0, len(level), 2)
                    ]
                inside = jnp.broadcast_to(wanted[side][2][p : p + 1], (8, 256)) > 0.5
                total = jnp.where(inside, level[0], 0.0)
                halves = jnp.concatenate(
                    [pltpu.roll(total[:, 128 * j : 128 * j + 128], 64, 1) for j in range(2)], axis=1
                )
                swapped = jnp.where(wide_row < 6, pltpu.roll(total, 3 if side else 5, 0), halves)
                chosen = jnp.where(jnp.abs(far - side) < 0.5, total, swapped)
                message = jnp.where(of_face[side], chosen, message)
            sy[p] = message

        @pl.when(y_special)
        def _():
            pl.semaphore_wait(ready, 1)

        for yy in range(ny):

            @pl.when(y != yy)
            def _():
                y_copy(yy, y).start()

        for zz in range(1, nz):

            @pl.when(between(zz, 80, 1000))
            def _():
                z_copy(zz, z).start()

        ry[y] = sy[y]

    @pl.when(late_line)
    def _():
        pl.semaphore_wait(ready, 1)

    for chunk in range(3):
        for i in range(7):

            @pl.when(is_late(i))
            def _():
                forward(chunk, i).start()

    loads[5].wait()
    nu = [coef[v] for v in range(5)]

    def y_pair(pair, nu_first, nu_second):
        nu_lane = STEP * jnp.where(lo, nu_first, nu_second)
        high, low = split(r_ab[pair])
        qcat[:, :128] = high
        qcat[:, 128:] = low
        res[...] = mm(yth[...], qcat[...])
        res2[...] = mm(ytl[...], qcat[:, :128])

        @pl.loop(0, 8)
        def _(i):
            a = pl.ds(pl.multiple_of(i * 64, 64), 64)
            b = pl.ds(pl.multiple_of(i * 64 + 512, 64), 64)
            dy = res[a, :128] + res[a, 128:] + res2[a]
            dyy = res[b, :128] + res[b, 128:] + res2[b]
            t_ab[pair, a] = nu_lane * dyy - vv[a] * dy

    for i in range(7):
        forward(0, i).wait_recv()
    start = r_ab[0]
    lo_all = lax.broadcasted_iota(jnp.int32, (512, 128), 1) < 64
    vv[...] = STEP * jnp.where(lo_all, start, pltpu.roll(start, 64, 1))
    y_pair(0, nu[1], nu[0])
    answer(0, 20, 0, 40)
    for i in range(7):
        backward(0, i).start()
    b_ab[0, line] = t_ab[0, here]

    for i in range(7):
        forward(1, i).wait_recv()
    y_pair(1, nu[2], nu[3])
    pl.when(jnp.logical_not(is_first))(lambda: answer(20, 45, 40, 1000))
    for i in range(7):
        backward(1, i).start()
    b_ab[1, line] = t_ab[1, here]

    for i in range(7):
        forward(2, i).wait_recv()
    for s in range(8):
        part = r_c[s]
        turned = pltpu.roll(part, 64, 1)
        for half, (keep, other) in enumerate(((part, turned), (turned, part))):
            high = keep.astype(BF16).astype(F32)
            low = other - other.astype(BF16).astype(F32)
            rows = slice(64 * s + 32 * half, 64 * s + 32 * half + 32)
            qcat[rows, :128] = jnp.where(lo32, high, low).astype(BF16)
    res2[...] = mm(yth[...], qcat[:, :128]) + mm(ytl[...], qcat[:, :128])

    @pl.loop(0, 8)
    def _(i):
        a = pl.ds(pl.multiple_of(i * 64, 64), 64)
        b = pl.ds(pl.multiple_of(i * 64 + 512, 64), 64)
        dy = res2[a] + pltpu.roll(res2[a], 64, 1)
        dyy = res2[b] + pltpu.roll(res2[b], 64, 1)
        term = (STEP * nu[4]) * dyy - vv[a] * dy
        t_c[i] = jnp.where(lo32, term[:32], term[32:])

    for i in range(7):
        backward(2, i).start()
    b_c[line] = t_c[line]
    pl.when(is_first)(lambda: ghost_stage(20))

    loads[8].wait()

    @pl.loop(0, 8)
    def _(i):
        rows = pl.ds(pl.multiple_of(i * 64, 64), 64)
        high, low = split(xop[rows])
        xh[rows] = high
        xl[rows] = low

    for v in range(5):
        high, low = split(m[v])
        mh[64 * v : 64 * v + 64] = high
        ml[64 * v : 64 * v + 64] = low
    for n in range(2):
        deriv = []
        for o in range(2):
            cols = slice(512 * o + 256 * n, 512 * o + 256 * n + 256)
            deriv.append(
                mm(mh[...], xh[:, cols])
                + mm(ml[...], xh[:, cols])
                + mm(mh[...], xl[:, cols])
            )
        cols = slice(256 * n, 256 * n + 256)
        u = STEP * m[0, :, cols]
        for v in range(5):
            rows = slice(64 * v, 64 * v + 64)
            term = m[v, :, cols] + (STEP * nu[v]) * deriv[1][rows] - u * deriv[0][rows]
            if v == 1:
                term = term + (STEP * coef[5]) * m[3, :, cols] + (STEP * coef[6]) * m[4, :, cols]
            acc[v, :, cols] = term

    pl.when(jnp.logical_not(is_first))(ghost_stage)

    for pair, (first, second) in enumerate(((1, 0), (2, 3))):
        for i in range(7):
            backward(pair, i).wait_recv()
        for c in range(4):
            cols = slice(128 * c, 128 * c + 128)
            a, b = b_ab[pair, 2 * c], b_ab[pair, 2 * c + 1]
            acc[first, :, cols] += jnp.where(lo, a, pltpu.roll(b, 64, 1))
            acc[second, :, cols] += jnp.where(lo, pltpu.roll(a, 64, 1), b)

    for chunk in range(3):
        for i in range(7):
            forward(chunk, i).wait_send()
            if chunk < 2:
                backward(chunk, i).wait_send()
    for zz in range(nz):

        @pl.when(z != zz)
        def _():
            z_copy(zz, z).wait_send()

    for yy in range(ny):

        @pl.when(y != yy)
        def _():
            y_copy(yy, yy).wait_recv()

    for yy in range(ny):

        @pl.when(y != yy)
        def _():
            y_copy(yy, y).wait_send()

    ghost = ry[0]
    for p in range(1, ny):
        ghost = ghost + ry[p]
    one, two = ghost[:, :128], ghost[:, 128:]
    row = plane_row[:, :128]
    last = jnp.where(row < 2, pltpu.roll(one, 2, 0), pltpu.roll(two, 4, 0))
    last = jnp.where((row == 3) | (row == 4), pltpu.roll(pltpu.roll(one, 64, 1), 5, 0), last)
    last = jnp.where(row == 5, pltpu.roll(pltpu.roll(two, 64, 1), 7, 0), last)
    ghost = jnp.concatenate([one, two, jnp.where(lanes[:8] < 64, last, 0.0)], axis=1)
    flip = jnp.where(plane_row < 3, 1.0 - own[0], own[1])
    turned = jnp.where(
        (plane_row == 0) | (plane_row == 3),
        pltpu.roll(ghost, 6, 0),
        jnp.where((plane_row == 2) | (plane_row == 5), pltpu.roll(ghost, 2, 0), ghost),
    )
    column = lax.broadcasted_iota(jnp.int32, (8, 384), 1)
    turned = jnp.where(column < 64, -turned, turned)
    ghost = jnp.where(flip > 0.5, turned, ghost)
    ghost = jnp.where(plane_row < 6, ghost, 0.0)
    ghost_high = ghost.astype(BF16).astype(F32)
    stack = jnp.concatenate([ghost_high, ghost - ghost_high, ghost_high, jnp.zeros((104, 384), F32)], axis=0)
    ghost_t = jnp.concatenate(
        [jnp.transpose(stack[:, 128 * j : 128 * j + 128]) for j in range(3)], axis=0
    )[:320].astype(BF16)
    for n in range(2):
        cols = slice(256 * n, 256 * n + 256)
        dx = mm(ghost_t, gstack[:, cols])
        dxx = mm(ghost_t, gstack[:, 256 * n + 512 : 256 * n + 768])
        u = STEP * m[0, :, cols]
        for v in range(5):
            rows = slice(64 * v, 64 * v + 64)
            term = acc[v, :, cols] + (STEP * nu[v]) * dxx[rows] - u * dx[rows]
            if v < 4:
                out[v, :, cols] = jnp.concatenate([live, live], axis=1) * term
            else:
                acc[v, :, cols] = term

    for i in range(7):
        backward(2, i).wait_recv()
    for c in range(4):
        cols = slice(128 * c, 128 * c + 128)
        a, b = b_c[2 * c], b_c[2 * c + 1]
        top = jnp.where(lo32, a, pltpu.roll(b, 64, 1))
        bottom = jnp.where(lo32, pltpu.roll(a, 64, 1), b)
        out[4, :32, cols] = live[:32] * (acc[4, :32, cols] + top)
        out[4, 32:, cols] = live[32:] * (acc[4, 32:, cols] + bottom)

    for i in range(7):
        backward(2, i).wait_send()


def on_device(
    nz,
    ny,
    flow_state,
    block_owner,
    link_block,
    link_side,
    rows_live,
    x_operator,
    ghost_operator,
    y_operator,
    coefficients,
):
    any_spec = pl.BlockSpec(memory_space=pltpu.HBM)
    dma = pltpu.SemaphoreType.DMA
    blocks = nz * ny
    result = pl.pallas_call(
        functools.partial(kernel, nz, ny, 111 if nz > 8 else 15 * nz + 3),
        out_shape=jax.ShapeDtypeStruct((5, 64, 512), F32),
        in_specs=[any_spec] * 9,
        out_specs=pl.BlockSpec(memory_space=pltpu.VMEM),
        scratch_shapes=[
            pltpu.VMEM((5, 64, 512), F32),
            pltpu.VMEM((1, blocks), jnp.int32),
            pltpu.VMEM((2, blocks), jnp.int32),
            pltpu.VMEM((2, blocks), jnp.int32),
            pltpu.VMEM((1, blocks), jnp.int32),
            pltpu.SMEM((7,), F32),
            pltpu.VMEM((6, 1024), F32),
            pltpu.VMEM((512, 1024), F32),
            pltpu.VMEM((512, 1024), F32),
            pltpu.VMEM((512, 1024), BF16),
            pltpu.VMEM((512, 1024), BF16),
            pltpu.VMEM((1024, 512), BF16),
            pltpu.VMEM((1024, 512), BF16),
            pltpu.VMEM((320, 512), BF16),
            pltpu.VMEM((320, 512), BF16),
            pltpu.VMEM((2, 8, 64, 128), F32),
            pltpu.VMEM((8, 32, 128), F32),
            pltpu.VMEM((2, 512, 128), F32),
            pltpu.VMEM((8, 32, 128), F32),
            pltpu.VMEM((2, 512, 128), F32),
            pltpu.VMEM((8, 32, 128), F32),
            pltpu.VMEM((2, 8, 64, 128), F32),
            pltpu.VMEM((8, 32, 128), F32),
            pltpu.VMEM((512, 128), F32),
            pltpu.VMEM((512, 256), BF16),
            pltpu.VMEM((1024, 256), F32),
            pltpu.VMEM((1024, 128), F32),
            pltpu.VMEM((5, 64, 512), F32),
            pltpu.VMEM((8, 256), F32),
            pltpu.VMEM((nz, 8, 256), F32),
            pltpu.VMEM((ny, 8, 256), F32),
            pltpu.VMEM((ny, 8, 256), F32),
            dma((9,)),
            dma((3, 7)),
            dma((3, 7)),
            dma((3, 7)),
            dma((3, 7)),
            dma((nz,)),
            dma((nz,)),
            dma((ny,)),
            dma((ny,)),
            pltpu.SemaphoreType.REGULAR,
            pltpu.VMEM((128, 1024), BF16),
        ],
        compiler_params=pltpu.CompilerParams(
            collective_id=0, has_side_effects=True, vmem_limit_bytes=40 * 1024 * 1024
        ),
        cost_estimate=pl.CostEstimate(flops=2 * 10**9, bytes_accessed=6 * 10**6, transcendentals=0),
    )(
        *(
            pltpu.with_memory_space_constraint(value, pltpu.HBM)
            for value in (
                flow_state[0],
                block_owner[None],
                link_block.T,
                link_side.T,
                rows_live[None],
                x_operator,
                ghost_operator,
                y_operator,
                coefficients,
            )
        )
    )
    return result[None]


def solution(mesh):
    blocks = mesh.shape["blk"]
    ny = min(NY, blocks // 2)
    return jax.shard_map(
        functools.partial(on_device, blocks // ny, ny),
        mesh=mesh,
        in_specs=(P("blk", None, "line", None), P(), P(), P(), P(), P(), P(), P(), P()),
        out_specs=P("blk", None, "line", None),
        check_vma=False,
    )
```

```python
import functools

import jax
import jax.numpy as jnp
from jax import lax
from jax.experimental import pallas as pl
from jax.experimental.pallas import tpu as pltpu
from jax.sharding import PartitionSpec as P

NY = 8
STEP = 0.3
MESH = pl.DeviceIdType.MESH
F32 = jnp.float32
BF16 = jnp.bfloat16
PEERS = ((1, 0), (3, 0), (1, 1), (3, 1), (2, 0), (2, 1), (0, 1))


def split(value):
    high = value.astype(BF16)
    return high, (value - high.astype(F32)).astype(BF16)


def mm(a, b):
    return jnp.dot(a, b, preferred_element_type=F32)


def kernel(
    nz,
    ny,
    z_late,
    flow,
    owner_h,
    link_block_h,
    link_side_h,
    rows_live_h,
    xop_h,
    gop_h,
    yop_h,
    coef_h,
    out,
    m,
    owner_v,
    link_block_v,
    link_side_v,
    rows_live_v,
    coef,
    gop,
    xop,
    yop,
    xh,
    xl,
    yth,
    ytl,
    mh,
    ml,
    s_ab,
    s_c,
    r_ab,
    r_c,
    t_ab,
    t_c,
    b_ab,
    b_c,
    vv,
    qcat,
    res,
    res2,
    acc,
    face,
    gz,
    sy,
    ry,
    load_sem,
    fs,
    fr,
    bs,
    br,
    zs,
    zr,
    ys,
    yr,
    ready,
    gstack,
):
    loads = [
        pltpu.make_async_copy(a, b, load_sem.at[i])
        for i, (a, b) in enumerate(
            (
                (rows_live_h, rows_live_v),
                (owner_h, owner_v),
                (flow, m),
                (link_block_h, link_block_v),
                (link_side_h, link_side_v),
                (coef_h, coef),
                (gop_h, gop),
                (yop_h, yop),
                (xop_h, xop),
            )
        )
    ]
    for load in loads:
        load.start()

    line = lax.axis_index("line")
    slot = lax.axis_index("blk")
    chip, core = line // 2, lax.rem(line, 2)
    z, y = slot // ny, lax.rem(slot, ny)

    def peer(ahead, other):
        return lax.rem(chip + ahead, 4) * 2 + lax.rem(core + other, 2)

    is_first = (slot == 0) & (line == 0)
    late_line = (slot == 0) & (line != 0)
    z_special = (y == 0) & (line == 0)
    y_special = (z == 0) & (line == 0) & (y != 0)

    def usual(zz):
        return jnp.where(zz < 8, 15 * zz, 88 + 4 * zz)

    my_z = jnp.where(is_first, z_late, usual(z))
    gaps = [jnp.where(z_special, z_late, 0) - my_z]
    gaps += [(15 * zz if zz < 8 else 88 + 4 * zz) - my_z for zz in range(1, nz)]
    close = [jnp.abs(gap) <= 10 for gap in gaps]
    close[0] = close[0] & jnp.logical_not(z_special)
    close = [here & jnp.logical_not(is_first) for here in close]
    now = [(z != zz) & ((gaps[zz] < 0) | close[zz]) for zz in range(nz)]

    barrier = pltpu.get_barrier_semaphore()

    @pl.when(jnp.logical_not(is_first))
    def _():
        for ahead, other in PEERS:
            pl.semaphore_signal(
                barrier, inc=1, device_id={"line": peer(ahead, other)}, device_id_type=MESH
            )

    waits = len(PEERS) - jnp.where(late_line, 1, 0) + ny - 1 - jnp.where(y_special, 1, 0)
    for zz in range(nz):
        waits += jnp.where(now[zz], 1, 0)

    for zz in range(nz):

        @pl.when((z != zz) & ((gaps[zz] > 0) | close[zz]))
        def _():
            pl.semaphore_signal(barrier, inc=1, device_id={"blk": zz * ny + y}, device_id_type=MESH)

    for yy in range(ny):

        @pl.when((y != yy) & jnp.logical_not(is_first))
        def _():
            pl.semaphore_signal(barrier, inc=1, device_id={"blk": z * ny + yy}, device_id_type=MESH)

    @pl.when(is_first)
    def _():
        pl.semaphore_wait(barrier, waits)
        for ahead, other in PEERS:
            pl.semaphore_signal(
                ready, inc=1, device_id={"line": peer(ahead, other)}, device_id_type=MESH
            )

        @pl.loop(1, ny)
        def _(yy):
            pl.semaphore_signal(ready, inc=1, device_id={"blk": z * ny + yy}, device_id_type=MESH)

    loads[0].wait()
    loads[1].wait()

    lanes = lax.broadcasted_iota(jnp.int32, (64, 128), 1)
    lo = lanes < 64
    mine = owner_v[...] == slot
    live_rows = jnp.sum(jnp.where(mine, rows_live_v[...].astype(F32), 0.0), axis=1, keepdims=True)
    row_id = (lax.broadcasted_iota(jnp.int32, (64, 128), 0) + line * 64).astype(F32)
    live = (row_id < live_rows).astype(F32)
    loads[2].wait()

    planes = []
    for v in range(5):
        low, high = m[v, :, 0:128], pltpu.roll(m[v, :, 384:512], 6, 1)
        planes.append(live * jnp.where(lanes < 3, low, high))
    last = planes[4]
    for v, moves in enumerate(((6, 6), (3, 3), (4, None), (1, None))):
        for lane, move in zip((6, 7), moves):
            if move is not None:
                planes[v] = jnp.where(lanes == lane, pltpu.roll(last, move, 1), planes[v])
    for j in range(2):
        both = jnp.concatenate([planes[2 * j], planes[2 * j + 1]], axis=0)
        face[:, 128 * j : 128 * j + 128] = jnp.transpose(both)[:8]

    @pl.when(jnp.logical_not(is_first))
    def _():
        pl.semaphore_wait(barrier, waits)

    here = pl.ds(pl.multiple_of(line * 64, 64), 64)

    def forward(chunk, i):
        ahead, other = PEERS[i]
        to = peer(ahead, other)
        if chunk < 2:
            source, target = s_ab.at[chunk, to], r_ab.at[chunk, here]
        else:
            source, target = s_c.at[to], r_c.at[line]
        return pltpu.make_async_remote_copy(
            src_ref=source,
            dst_ref=target,
            send_sem=fs.at[chunk, i],
            recv_sem=fr.at[chunk, i],
            device_id={"line": to},
            device_id_type=MESH,
        )

    def backward(chunk, i):
        ahead, other = PEERS[i]
        to = peer(ahead, other)
        if chunk < 2:
            source = t_ab.at[chunk, pl.ds(pl.multiple_of(to * 64, 64), 64)]
            target = b_ab.at[chunk, line]
        else:
            source, target = t_c.at[to], b_c.at[line]
        return pltpu.make_async_remote_copy(
            src_ref=source,
            dst_ref=target,
            send_sem=bs.at[chunk, i],
            recv_sem=br.at[chunk, i],
            device_id={"line": to},
            device_id_type=MESH,
        )

    def z_copy(zz, sender):
        return pltpu.make_async_remote_copy(
            src_ref=face,
            dst_ref=gz.at[sender],
            send_sem=zs.at[zz],
            recv_sem=zr.at[sender],
            device_id={"blk": zz * ny + y},
            device_id_type=MESH,
        )

    def y_copy(yy, sender):
        return pltpu.make_async_remote_copy(
            src_ref=sy.at[yy],
            dst_ref=ry.at[sender],
            send_sem=ys.at[yy],
            recv_sem=yr.at[sender],
            device_id={"blk": z * ny + yy},
            device_id_type=MESH,
        )

    def is_late(i):
        return late_line & (peer(*PEERS[i]) == 0)

    def send_forward(chunk, i):
        @pl.when(jnp.logical_not(is_late(i)))
        def _():
            forward(chunk, i).start()

    for zz in range(nz):

        @pl.when(now[zz] if zz < 8 else now[zz] & (z < 8))
        def _():
            z_copy(zz, z).start()

    def pack(pair, first, second):
        for c in range(4):
            cols = slice(128 * c, 128 * c + 128)
            a = m[first, :, cols] * live
            b = m[second, :, cols] * live
            m[first, :, cols] = a
            m[second, :, cols] = b
            s_ab[pair, 2 * c] = jnp.where(lo, a, pltpu.roll(b, 64, 1))
            s_ab[pair, 2 * c + 1] = jnp.where(lo, pltpu.roll(a, 64, 1), b)
    pack(0, 1, 0)
    for i in range(7):
        send_forward(0, i)
    pack(1, 2, 3)
    for i in range(7):
        send_forward(1, i)
    lo32 = lo[:32]
    for c in range(4):
        cols = slice(128 * c, 128 * c + 128)
        a = m[4, :, cols] * live
        m[4, :, cols] = a
        s_c[2 * c] = jnp.where(lo32, a[:32], pltpu.roll(a[32:], 64, 1))
        s_c[2 * c + 1] = jnp.where(lo32, pltpu.roll(a[:32], 64, 1), a[32:])

    for i in range(7):
        send_forward(2, i)
    for zz in range(8, nz):

        @pl.when(now[zz] & (z >= 8))
        def _():
            z_copy(zz, z).start()

    gz[z] = face[...]
    r_ab[0, here] = s_ab[0, line]
    r_ab[1, here] = s_ab[1, line]
    r_c[line] = s_c[line]

    loads[7].wait()

    @pl.loop(0, 8)
    def _(i):
        rows = pl.ds(pl.multiple_of(i * 128, 128), 128)
        for j in range(4):
            block = jnp.transpose(yop[128 * j : 128 * j + 128, rows])
            high, low = split(block)
            yth[rows, 128 * j : 128 * j + 128] = high
            ytl[rows, 128 * j : 128 * j + 128] = low

    loads[3].wait()
    loads[4].wait()
    peers_row = lax.broadcasted_iota(jnp.int32, (ny, nz * ny), 0) + z * ny
    lane_row = lax.broadcasted_iota(jnp.int32, (ny, nz * ny), 1).astype(F32)
    owner = owner_v[...]
    owner_f = owner.astype(F32)
    hot = owner == peers_row
    wanted = []
    for side in range(2):
        partner = jnp.sum(
            jnp.where(hot, link_block_v[side : side + 1, :].astype(F32), 0.0), axis=1, keepdims=True
        )
        far = jnp.sum(
            jnp.where(hot, link_side_v[side : side + 1, :].astype(F32), 0.0), axis=1, keepdims=True
        )
        source = jnp.sum(jnp.where(lane_row == partner, owner_f, 0.0), axis=1, keepdims=True)
        source = source.astype(jnp.int32)
        source_z = source // ny
        bits = []
        while 2 ** len(bits) < nz:
            bits.append((source_z // 2 ** len(bits) % 2).astype(F32))
        wanted.append((bits, far, (source % ny == y).astype(F32)))

    own = []
    for side in range(2):
        own.append(
            jnp.sum(jnp.where(mine, link_side_v[side : side + 1, :].astype(F32), 0.0), axis=1, keepdims=True)
        )

    loads[6].wait()
    g_op = jnp.concatenate([gop[...], jnp.zeros((2, 1024), F32)], axis=0)
    g_high = g_op.astype(BF16).astype(F32)
    gstack[...] = jnp.concatenate(
        [g_high, g_high, g_op - g_high, jnp.zeros((104, 1024), F32)], axis=0
    ).astype(BF16)

    plane_row = lax.broadcasted_iota(jnp.int32, (8, 384), 0)
    wide_row = plane_row[:, :256]
    half = lax.rem(lax.broadcasted_iota(jnp.int32, (8, 256), 1), 128) // 64
    of_face = [
        ((wide_row >= 3 * f) & (wide_row < 3 * f + 3)) | ((wide_row >= 6) & (half == f))
        for f in range(2)
    ]

    def between(zz, least, most):
        return (gaps[zz] > least) & (gaps[zz] <= most) & jnp.logical_not(close[zz])

    order = (*range(1, min(8, nz)), 0, *range(8, nz))

    def answer(least, most, first_least, first_most):
        for zz in order:

            @pl.when(between(zz, least, most) if zz else between(zz, first_least, first_most))
            def _():
                z_copy(zz, zz).wait_recv()
                z_copy(zz, z).start()

    def ghost_stage(least=45):
        for zz in range(1, nz):

            @pl.when(between(zz, least, 1000))
            def _():
                z_copy(zz, zz).wait_recv()

            @pl.when(between(zz, least, 80))
            def _():
                z_copy(zz, z).start()

        for zz in range(nz):

            @pl.when(now[zz])
            def _():
                z_copy(zz, zz).wait_recv()

        for p in range(ny):
            message = jnp.zeros((8, 256), F32)
            for side in range(2):
                far = jnp.broadcast_to(wanted[side][1][p : p + 1], (8, 256))
                level = [gz[zz] for zz in range(nz)]
                for bits in wanted[side][0]:
                    bit = jnp.broadcast_to(bits[p : p + 1], (8, 256)) > 0.5
                    level = [
                        jnp.where(bit, level[k + 1], level[k]) for k in range(0, len(level), 2)
                    ]
                inside = jnp.broadcast_to(wanted[side][2][p : p + 1], (8, 256)) > 0.5
                total = jnp.where(inside, level[0], 0.0)
                halves = jnp.concatenate(
                    [pltpu.roll(total[:, 128 * j : 128 * j + 128], 64, 1) for j in range(2)], axis=1
                )
                swapped = jnp.where(wide_row < 6, pltpu.roll(total, 3 if side else 5, 0), halves)
                chosen = jnp.where(jnp.abs(far - side) < 0.5, total, swapped)
                message = jnp.where(of_face[side], chosen, message)
            sy[p] = message

        @pl.when(y_special)
        def _():
            pl.semaphore_wait(ready, 1)

        for yy in range(ny):

            @pl.when(y != yy)
            def _():
                y_copy(yy, y).start()

        for zz in range(1, nz):

            @pl.when(between(zz, 80, 1000))
            def _():
                z_copy(zz, z).start()

        ry[y] = sy[y]

    @pl.when(late_line)
    def _():
        pl.semaphore_wait(ready, 1)

    for chunk in range(3):
        for i in range(7):

            @pl.when(is_late(i))
            def _():
                forward(chunk, i).start()

    loads[5].wait()
    nu = [coef[v] for v in range(5)]

    def y_pair(pair, nu_first, nu_second):
        nu_lane = STEP * jnp.where(lo, nu_first, nu_second)
        high, low = split(r_ab[pair])
        qcat[:, :128] = high
        qcat[:, 128:] = low
        res[...] = mm(yth[...], qcat[...])
        res2[...] = mm(ytl[...], qcat[:, :128])

        @pl.loop(0, 8)
        def _(i):
            a = pl.ds(pl.multiple_of(i * 64, 64), 64)
            b = pl.ds(pl.multiple_of(i * 64 + 512, 64), 64)
            dy = res[a, :128] + res[a, 128:] + res2[a]
            dyy = res[b, :128] + res[b, 128:] + res2[b]
            t_ab[pair, a] = nu_lane * dyy - vv[a] * dy

    for i in range(7):
        forward(0, i).wait_recv()
    start = r_ab[0]
    lo_all = lax.broadcasted_iota(jnp.int32, (512, 128), 1) < 64
    vv[...] = STEP * jnp.where(lo_all, start, pltpu.roll(start, 64, 1))
    y_pair(0, nu[1], nu[0])
    answer(0, 20, 0, 40)
    for i in range(7):
        backward(0, i).start()
    b_ab[0, line] = t_ab[0, here]

    for i in range(7):
        forward(1, i).wait_recv()
    y_pair(1, nu[2], nu[3])
    pl.when(jnp.logical_not(is_first))(lambda: answer(20, 45, 40, 1000))
    for i in range(7):
        backward(1, i).start()
    b_ab[1, line] = t_ab[1, here]

    for i in range(7):
        forward(2, i).wait_recv()
    for s in range(8):
        part = r_c[s]
        turned = pltpu.roll(part, 64, 1)
        for half, (keep, other) in enumerate(((part, turned), (turned, part))):
            high = keep.astype(BF16).astype(F32)
            low = other - other.astype(BF16).astype(F32)
            rows = slice(64 * s + 32 * half, 64 * s + 32 * half + 32)
            qcat[rows, :128] = jnp.where(lo32, high, low).astype(BF16)
    res2[...] = mm(yth[...], qcat[:, :128]) + mm(ytl[...], qcat[:, :128])

    @pl.loop(0, 8)
    def _(i):
        a = pl.ds(pl.multiple_of(i * 64, 64), 64)
        b = pl.ds(pl.multiple_of(i * 64 + 512, 64), 64)
        dy = res2[a] + pltpu.roll(res2[a], 64, 1)
        dyy = res2[b] + pltpu.roll(res2[b], 64, 1)
        term = (STEP * nu[4]) * dyy - vv[a] * dy
        t_c[i] = jnp.where(lo32, term[:32], term[32:])

    for i in range(7):
        backward(2, i).start()
    b_c[line] = t_c[line]
    pl.when(is_first)(lambda: ghost_stage(20))

    loads[8].wait()

    @pl.loop(0, 8)
    def _(i):
        rows = pl.ds(pl.multiple_of(i * 64, 64), 64)
        high, low = split(xop[rows])
        xh[rows] = high
        xl[rows] = low

    for v in range(5):
        high, low = split(m[v])
        mh[64 * v : 64 * v + 64] = high
        ml[64 * v : 64 * v + 64] = low
    for n in range(2):
        deriv = []
        for o in range(2):
            cols = slice(512 * o + 256 * n, 512 * o + 256 * n + 256)
            deriv.append(
                mm(mh[...], xh[:, cols])
                + mm(ml[...], xh[:, cols])
                + mm(mh[...], xl[:, cols])
            )
        cols = slice(256 * n, 256 * n + 256)
        u = STEP * m[0, :, cols]
        for v in range(5):
            rows = slice(64 * v, 64 * v + 64)
            term = m[v, :, cols] + (STEP * nu[v]) * deriv[1][rows] - u * deriv[0][rows]
            if v == 1:
                term = term + (STEP * coef[5]) * m[3, :, cols] + (STEP * coef[6]) * m[4, :, cols]
            acc[v, :, cols] = term

    pl.when(jnp.logical_not(is_first))(ghost_stage)

    for pair, (first, second) in enumerate(((1, 0), (2, 3))):
        for i in range(7):
            backward(pair, i).wait_recv()
        for c in range(4):
            cols = slice(128 * c, 128 * c + 128)
            a, b = b_ab[pair, 2 * c], b_ab[pair, 2 * c + 1]
            acc[first, :, cols] += jnp.where(lo, a, pltpu.roll(b, 64, 1))
            acc[second, :, cols] += jnp.where(lo, pltpu.roll(a, 64, 1), b)

    for yy in range(ny):

        @pl.when(y != yy)
        def _():
            y_copy(yy, yy).wait_recv()

    ghost = ry[0]
    for p in range(1, ny):
        ghost = ghost + ry[p]
    one, two = ghost[:, :128], ghost[:, 128:]
    row = plane_row[:, :128]
    last = jnp.where(row < 2, pltpu.roll(one, 2, 0), pltpu.roll(two, 4, 0))
    last = jnp.where((row == 3) | (row == 4), pltpu.roll(pltpu.roll(one, 64, 1), 5, 0), last)
    last = jnp.where(row == 5, pltpu.roll(pltpu.roll(two, 64, 1), 7, 0), last)
    ghost = jnp.concatenate([one, two, jnp.where(lanes[:8] < 64, last, 0.0)], axis=1)
    flip = jnp.where(plane_row < 3, 1.0 - own[0], own[1])
    turned = jnp.where(
        (plane_row == 0) | (plane_row == 3),
        pltpu.roll(ghost, 6, 0),
        jnp.where((plane_row == 2) | (plane_row == 5), pltpu.roll(ghost, 2, 0), ghost),
    )
    column = lax.broadcasted_iota(jnp.int32, (8, 384), 1)
    turned = jnp.where(column < 64, -turned, turned)
    ghost = jnp.where(flip > 0.5, turned, ghost)
    ghost = jnp.where(plane_row < 6, ghost, 0.0)
    ghost_high = ghost.astype(BF16).astype(F32)
    stack = jnp.concatenate([ghost_high, ghost - ghost_high, ghost_high, jnp.zeros((104, 384), F32)], axis=0)
    ghost_t = jnp.concatenate(
        [jnp.transpose(stack[:, 128 * j : 128 * j + 128]) for j in range(3)], axis=0
    )[:320].astype(BF16)
    for n in range(2):
        cols = slice(256 * n, 256 * n + 256)
        dx = mm(ghost_t, gstack[:, cols])
        dxx = mm(ghost_t, gstack[:, 256 * n + 512 : 256 * n + 768])
        u = STEP * m[0, :, cols]
        for v in range(5):
            rows = slice(64 * v, 64 * v + 64)
            term = acc[v, :, cols] + (STEP * nu[v]) * dxx[rows] - u * dx[rows]
            if v < 4:
                out[v, :, cols] = jnp.concatenate([live, live], axis=1) * term
            else:
                acc[v, :, cols] = term

    for i in range(7):
        backward(2, i).wait_recv()
    for c in range(4):
        cols = slice(128 * c, 128 * c + 128)
        a, b = b_c[2 * c], b_c[2 * c + 1]
        top = jnp.where(lo32, a, pltpu.roll(b, 64, 1))
        bottom = jnp.where(lo32, pltpu.roll(a, 64, 1), b)
        out[4, :32, cols] = live[:32] * (acc[4, :32, cols] + top)
        out[4, 32:, cols] = live[32:] * (acc[4, 32:, cols] + bottom)

    for chunk in range(3):
        for i in range(7):
            forward(chunk, i).wait_send()
            if chunk < 2:
                backward(chunk, i).wait_send()
    for zz in range(nz):

        @pl.when(z != zz)
        def _():
            z_copy(zz, z).wait_send()

    for yy in range(ny):

        @pl.when(y != yy)
        def _():
            y_copy(yy, y).wait_send()

    for i in range(7):
        backward(2, i).wait_send()


def on_device(
    nz,
    ny,
    flow_state,
    block_owner,
    link_block,
    link_side,
    rows_live,
    x_operator,
    ghost_operator,
    y_operator,
    coefficients,
):
    any_spec = pl.BlockSpec(memory_space=pltpu.HBM)
    dma = pltpu.SemaphoreType.DMA
    blocks = nz * ny
    result = pl.pallas_call(
        functools.partial(kernel, nz, ny, 111 if nz > 8 else 15 * nz + 3),
        out_shape=jax.ShapeDtypeStruct((5, 64, 512), F32),
        in_specs=[any_spec] * 9,
        out_specs=pl.BlockSpec(memory_space=pltpu.VMEM),
        scratch_shapes=[
            pltpu.VMEM((5, 64, 512), F32),
            pltpu.VMEM((1, blocks), jnp.int32),
            pltpu.VMEM((2, blocks), jnp.int32),
            pltpu.VMEM((2, blocks), jnp.int32),
            pltpu.VMEM((1, blocks), jnp.int32),
            pltpu.SMEM((7,), F32),
            pltpu.VMEM((6, 1024), F32),
            pltpu.VMEM((512, 1024), F32),
            pltpu.VMEM((512, 1024), F32),
            pltpu.VMEM((512, 1024), BF16),
            pltpu.VMEM((512, 1024), BF16),
            pltpu.VMEM((1024, 512), BF16),
            pltpu.VMEM((1024, 512), BF16),
            pltpu.VMEM((320, 512), BF16),
            pltpu.VMEM((320, 512), BF16),
            pltpu.VMEM((2, 8, 64, 128), F32),
            pltpu.VMEM((8, 32, 128), F32),
            pltpu.VMEM((2, 512, 128), F32),
            pltpu.VMEM((8, 32, 128), F32),
            pltpu.VMEM((2, 512, 128), F32),
            pltpu.VMEM((8, 32, 128), F32),
            pltpu.VMEM((2, 8, 64, 128), F32),
            pltpu.VMEM((8, 32, 128), F32),
            pltpu.VMEM((512, 128), F32),
            pltpu.VMEM((512, 256), BF16),
            pltpu.VMEM((1024, 256), F32),
            pltpu.VMEM((1024, 128), F32),
            pltpu.VMEM((5, 64, 512), F32),
            pltpu.VMEM((8, 256), F32),
            pltpu.VMEM((nz, 8, 256), F32),
            pltpu.VMEM((ny, 8, 256), F32),
            pltpu.VMEM((ny, 8, 256), F32),
            dma((9,)),
            dma((3, 7)),
            dma((3, 7)),
            dma((3, 7)),
            dma((3, 7)),
            dma((nz,)),
            dma((nz,)),
            dma((ny,)),
            dma((ny,)),
            pltpu.SemaphoreType.REGULAR,
            pltpu.VMEM((128, 1024), BF16),
        ],
        compiler_params=pltpu.CompilerParams(
            collective_id=0, has_side_effects=True, vmem_limit_bytes=40 * 1024 * 1024
        ),
        cost_estimate=pl.CostEstimate(flops=2 * 10**9, bytes_accessed=6 * 10**6, transcendentals=0),
    )(
        *(
            pltpu.with_memory_space_constraint(value, pltpu.HBM)
            for value in (
                flow_state[0],
                block_owner[None],
                link_block.T,
                link_side.T,
                rows_live[None],
                x_operator,
                ghost_operator,
                y_operator,
                coefficients,
            )
        )
    )
    return result[None]


def solution(mesh):
    blocks = mesh.shape["blk"]
    ny = min(NY, blocks // 2)
    return jax.shard_map(
        functools.partial(on_device, blocks // ny, ny),
        mesh=mesh,
        in_specs=(P("blk", None, "line", None), P(), P(), P(), P(), P(), P(), P(), P()),
        out_specs=P("blk", None, "line", None),
        check_vma=False,
    )
```
